128 devices in a mesh: ves: 32 (over z, x, core), deg: 4 (over y).
Axes of the slice: x: 4, y: 4, z: 4, core: 2. Of those that a mesh axis runs over, the one named last changes fastest.
Arguments:
- adj_velocity: bfloat16 [4096, 3, 544], P(('ves', 'deg')), may hold values from -6 to 6
- jacobian: bfloat16 [4096, 544], P(('ves', 'deg')), may hold values from 0.5 to 2
- self_kernel: bfloat16 [544, 544], replicated, may hold values from -0.25 to 0.25
- near_kernel_up: bfloat16 [544, 2112], replicated, may hold values from -0.25 to 0.25
- near_kernel_down: bfloat16 [2112, 544], replicated, may hold values from -0.125 to 0.125
- radial: float32 [2112], replicated, may hold values from 0.2 to 3
- near_dist: float32 [4096, 8], P(('ves', 'deg')), may hold values from 0.3 to 4
- near_owner: int32 [4096, 8], P(('ves', 'deg')), may hold values from 0 to 127, all different within a row; in each aligned block of 32 rows (0 to 31, 32 to 63, ...) at most 3 rows name the same one
- near_local: int32 [4096, 8], P(('ves', 'deg')), may hold values from 0 to 31
- live_pairs: int32 [128], P(('ves', 'deg')), may hold values from 64 to 256, as said below
- analysis: float32 [544, 288], replicated, may hold values from -0.25 to 0.25
- blocks: float32 [16, 3, 3, 4096], P('deg', None, None, 'ves'), as said below
Outputs:
- adj_coefficients: float32 [3, 288, 4096], P(None, 'deg', 'ves')
The draws below stay inside these ranges and needn't reach their ends.
Inputs may be any that keep to these rules, and one draw needn't show every extreme that they name: `near_owner`: each row names 8 different devices. Among the rows of one device's 32 vesicles no device is named more than 3 times, and some device is named exactly 3 times. `live_pairs`: each device has at least a quarter of its slots live, and some device has all 256 live. `blocks`: each 3 x 3 block is strictly diagonally dominant by rows, with positive diagonal.
All inputs are finite; a program needn't handle non-finite values.
Results may differ from the reference program's by a relative error of at most 0.0041.
Values may be sent and summed in bfloat16 or wider, within the bound.
No kernel may reach another device: no remote copies, remote signals or barrier semaphores. Data moves between devices by JAX's collectives and lax.ppermute only.
A program may use at most 64 MiB of HBM per device.

```python
import math
import jax
import jax.numpy as jnp
import numpy as np
from jax import lax

ORDER = 16
POINTS = 544
FINE_POINTS = 2112
COEFS = 288
VES_DEV = 32
NEAR = 8
CAP = 3
VESICLES = 4096
DEVICES = 128


def draw_live_pairs(key, part):
    key = jax.random.fold_in(key, 11)
    first, second = jax.random.split(key)
    total = VES_DEV * NEAR
    counts = jax.random.randint(first, (DEVICES,), total // 4, total + 1, dtype=jnp.int32)
    chosen = jax.random.randint(second, (), 0, DEVICES, dtype=jnp.int32)
    return jnp.where(jnp.arange(DEVICES, dtype=jnp.int32) == chosen, total, counts).astype(jnp.int32)


def draw_blocks(key, part):
    key = jax.random.fold_in(key, 23)
    first, second = jax.random.split(key)
    shape = (ORDER, 3, 3, VES_DEV * DEVICES)
    offdiag = jax.random.uniform(first, shape, jnp.float32, -0.45, 0.45)
    diagonal = jax.random.uniform(second, shape, jnp.float32, 1.5, 3.0)
    identity = jnp.eye(3, dtype=jnp.float32)[None, :, :, None]
    return offdiag * (1.0 - identity) + diagonal * identity


def plant(values, own_key, low, largest):
    longest = values.shape.index(max(values.shape))
    spots = []
    for shift in (0, 1):
        where = [jax.random.randint(jax.random.fold_in(own_key, axis), (), 0, length) for axis, length in enumerate(values.shape)]
        where[longest] = (where[longest] + shift) % values.shape[longest]
        spots.append(tuple(where))
    return values.at[spots[0]].set(low).at[spots[1]].set(largest)


def block_scale(rng, extent, shards, least, top_value):
    def one(dim, parts):
        draws = jax.random.uniform(jax.random.fold_in(jax.random.fold_in(rng, 6), dim), (parts,), jnp.float32, least / len(shards), top_value / len(shards))
        return jnp.repeat(jnp.exp(draws), extent[dim] // parts).reshape((-1,) + (1,) * (len(extent) - dim - 1))

    gain = one(*shards[0])
    for cut in shards[1:]:
        gain = gain * one(*cut)
    return gain


def shared_out(key, own, number, rows, count, top, most, lean):
    sequence = jax.random.permutation(key, count)
    crowded, common = portions_of(count, rows * top, most, lean, True), portions_of(count, rows * top, most, lean, False)
    places = jnp.arange(count)

    def named(sizes, turn):
        used = int((sizes > 0).sum())
        fixed = max(1, used // 4)
        moved = fixed + (places - fixed + turn * (used - fixed)) % max(1, count - fixed)
        return jnp.zeros((count,), jnp.int32).at[sequence[jnp.where(places < fixed, places, moved)]].set(jnp.asarray(sizes, jnp.int32))

    sizes = jnp.where(number % 4 == 0, named(crowded, number // 4), named(common, number - number // 4 - 1))
    mixed = jax.random.permutation(jax.random.fold_in(own, 3), count)
    donor, sink = mixed[0:count // 2 * 2:2], mixed[1:count // 2 * 2:2]
    margin = jnp.minimum(sizes[donor] - 1, most - sizes[sink]) // 2
    margin = jnp.where((donor == sequence[0]) | (sink == sequence[0]) | (sizes[sink] == 0), 0, jnp.maximum(margin, 0))
    moved = jax.random.randint(jax.random.fold_in(own, 4), (count // 2,), 0, 1 << 20) % (margin + 1)
    sizes = sizes.at[donor].add(-moved).at[sink].add(moved)
    members = jnp.searchsorted(jnp.cumsum(sizes), jnp.arange(rows * top), side="right").astype(jnp.int32)
    listing = members.reshape(top, rows).T
    listing = listing[jax.random.permutation(jax.random.fold_in(own, 1), rows)]
    turn = jax.random.randint(jax.random.fold_in(own, 2), (rows, 1), 0, top)
    return jnp.take_along_axis(listing, (jnp.arange(top)[None, :] + turn) % top, axis=1)


def portions_of(count, total, most, slope, full):
    portions = [(1 << 20) // math.isqrt(standing ** slope) + 1 for standing in range(1, count + 1)]
    largest = most if full else min(most, max(-(-total // count), total * portions[0] // sum(portions)))
    least = 1 if total - largest >= count - 1 else 0
    given, surplus = [largest] + [least] * (count - 1), total - largest - least * (count - 1)
    while surplus > 0:
        movable = [i for i in range(1, count) if given[i] < largest] or [i for i in range(1, count) if given[i] < most]
        pool, budget = sum([portions[i] for i in movable]), surplus
        for i in movable:
            extra = min(most - given[i], max(1, budget * portions[i] // pool), surplus)
            given[i] = given[i] + extra
            surplus = surplus - extra
    return np.array(given)


def gaussian(stream_key, dims, width, limit, shards=(), kind=jnp.bfloat16):
    factor_of = block_scale(stream_key, dims, shards, -0.22, 0.18) if shards else 1.0
    entries = jax.random.normal(stream_key, dims, jnp.float32) * width * factor_of
    return jnp.minimum(jnp.maximum(entries, -limit), limit).astype(kind)


def setup_inputs(seed: int = 0) -> dict:
    splits = jax.random.split(jax.random.key(seed), 13)
    adj_velocity = gaussian(splits[0], (VESICLES, 3, POINTS), 1.0, 6.0, ((0, 128),))
    jacobian = jnp.clip(jnp.exp(math.log(2.0) - 1.3862944 * jax.random.uniform(splits[1], (VESICLES, POINTS), jnp.float32) ** block_scale(splits[1], (VESICLES, POINTS), ((0, 128),), -0.2, 0.2)), 0.5, 2.0).astype(jnp.bfloat16)
    self_kernel = gaussian(splits[2], (POINTS, POINTS), POINTS ** -0.5, 0.25)
    near_kernel_up = gaussian(splits[3], (POINTS, FINE_POINTS), POINTS ** -0.5, 0.25)
    near_kernel_down = gaussian(splits[4], (FINE_POINTS, POINTS), FINE_POINTS ** -0.5, 0.125)
    radial = jnp.clip(jnp.exp(jax.random.uniform(splits[5], (FINE_POINTS,), jnp.float32, math.log(0.2), math.log(3.0))), 0.2, 3.0)
    near_dist = jnp.clip(jnp.exp(math.log(4.0) - 2.5902671 * jax.random.uniform(splits[6], (VESICLES, NEAR), jnp.float32) ** block_scale(splits[6], (VESICLES, NEAR), ((0, 128),), -0.2, 0.2)), 0.3, 4.0)
    near_owner_keys = jax.random.split(jax.random.fold_in(splits[7], 1), VESICLES // VES_DEV)
    near_owner_turns = jax.random.permutation(jax.random.fold_in(splits[7], 3), VESICLES // VES_DEV)
    near_owner = jax.vmap(lambda own, number: shared_out(jax.random.fold_in(splits[7], 2), own, number, VES_DEV, DEVICES, NEAR, CAP, 2))(near_owner_keys, near_owner_turns).reshape((VESICLES, NEAR))
    near_local = plant(jax.random.randint(splits[8], (VESICLES, NEAR), 0, VES_DEV), jax.random.fold_in(splits[8], 1), 0, VES_DEV - 1).astype(jnp.int32)
    live_pairs = draw_live_pairs(jax.random.fold_in(splits[12], 71), 0)
    analysis = gaussian(splits[10], (POINTS, COEFS), POINTS ** -0.5, 0.25, (), jnp.float32)
    blocks = draw_blocks(jax.random.fold_in(splits[12], 71), 0)
    return dict(adj_velocity=adj_velocity, jacobian=jacobian, self_kernel=self_kernel, near_kernel_up=near_kernel_up, near_kernel_down=near_kernel_down, radial=radial, near_dist=near_dist, near_owner=near_owner, near_local=near_local, live_pairs=live_pairs, analysis=analysis, blocks=blocks)


def coefficient_slots(order):
    widths = []
    for position in range(order // 2):
        widths.append(2 * position + 3)
        widths.append(2 * (order - position) + 1)
    return np.repeat(np.arange(order), np.array(widths))


def solve_three(matrix, rhs):
    cofactor = [
        [matrix[1][1] * matrix[2][2] - matrix[1][2] * matrix[2][1],
         matrix[1][2] * matrix[2][0] - matrix[1][0] * matrix[2][2],
         matrix[1][0] * matrix[2][1] - matrix[1][1] * matrix[2][0]],
        [matrix[0][2] * matrix[2][1] - matrix[0][1] * matrix[2][2],
         matrix[0][0] * matrix[2][2] - matrix[0][2] * matrix[2][0],
         matrix[0][1] * matrix[2][0] - matrix[0][0] * matrix[2][1]],
        [matrix[0][1] * matrix[1][2] - matrix[0][2] * matrix[1][1],
         matrix[0][2] * matrix[1][0] - matrix[0][0] * matrix[1][2],
         matrix[0][0] * matrix[1][1] - matrix[0][1] * matrix[1][0]],
    ]
    determinant = matrix[0][0] * cofactor[0][0] + matrix[0][1] * cofactor[0][1] + matrix[0][2] * cofactor[0][2]
    return jnp.stack([(cofactor[0][col] * rhs[0] + cofactor[1][col] * rhs[1] + cofactor[2][col] * rhs[2]) / determinant for col in range(3)])


def reference(adj_velocity, jacobian, self_kernel, near_kernel_up, near_kernel_down, radial, near_dist, near_owner, near_local, live_pairs, analysis, blocks):
    total_ves = VES_DEV * DEVICES
    scaled = (adj_velocity.astype(jnp.float32) * jacobian.astype(jnp.float32)[:, None, :]).astype(jnp.bfloat16)
    self_term = jnp.dot(scaled.reshape(-1, POINTS), self_kernel, preferred_element_type=jnp.float32).reshape(total_ves, 3, POINTS)

    def one_device(near_sum, device):
        start = (device * VES_DEV).astype(jnp.int32)
        adj_block = lax.dynamic_slice_in_dim(adj_velocity, start, VES_DEV, 0)
        dist_block = lax.dynamic_slice_in_dim(near_dist, start, VES_DEV, 0)
        owner_block = lax.dynamic_slice_in_dim(near_owner, start, VES_DEV, 0)
        local_block = lax.dynamic_slice_in_dim(near_local, start, VES_DEV, 0)
        live_count = lax.dynamic_index_in_dim(live_pairs, device, 0, keepdims=False)
        upsampled = jnp.dot(adj_block.reshape(-1, POINTS), near_kernel_up, preferred_element_type=jnp.float32).reshape(VES_DEV, 3, FINE_POINTS)
        weights = 1.0 / (1.0 + dist_block[:, :, None] * radial[None, None, :])
        field = (upsampled[:, None] * weights[:, :, None]).astype(jnp.bfloat16)
        partial_value = jnp.dot(field.reshape(-1, FINE_POINTS), near_kernel_down, preferred_element_type=jnp.float32).reshape(VES_DEV, NEAR, 3, POINTS)
        rows = jnp.arange(VES_DEV * NEAR, dtype=jnp.int32).reshape(VES_DEV, NEAR)
        live = rows < live_count
        partial_value = jnp.where(live[:, :, None, None], partial_value, jnp.zeros_like(partial_value))
        source = (owner_block * VES_DEV + local_block).astype(jnp.int32)
        near_sum = near_sum.at[source.reshape(-1)].add(partial_value.reshape(-1, 3, POINTS))
        return near_sum, None

    near_sum, unused = lax.scan(one_device, jnp.zeros((total_ves, 3, POINTS), jnp.float32), jnp.arange(DEVICES, dtype=jnp.int32))
    coef = jnp.einsum("vcp,pk->ckv", self_term + near_sum, analysis, precision=lax.Precision.HIGHEST)
    coef = lax.optimization_barrier(coef.astype(jnp.bfloat16)).astype(jnp.float32)
    slots = jnp.asarray(coefficient_slots(ORDER), dtype=jnp.int32)
    expanded = jnp.take(blocks, slots, axis=0)
    matrix = [[expanded[:, row, col, :] for col in range(3)] for row in range(3)]
    return solve_three(matrix, coef)
```

```python
import functools

import jax
import jax.numpy as jnp
import numpy as np
from jax import lax
from jax.experimental import pallas as pl
from jax.experimental.pallas import tpu as pltpu
from jax.sharding import PartitionSpec as P

VMEM = pltpu.CompilerParams(vmem_limit_bytes=56 * 1024 * 1024)
LANES = 128
NN = (((1,), (0,)), ((), ()))
NT = (((1,), (1,)), ((), ()))
TN = (((0,), (0,)), ((), ()))


def mm(a, b, dims=NN):
    return lax.dot_general(a, b, dims, preferred_element_type=jnp.float32)


def split(x):
    high = x.astype(jnp.bfloat16)
    return high, (x - high.astype(jnp.float32)).astype(jnp.bfloat16)


def columns(x, count):
    return jnp.concatenate(
        [jnp.broadcast_to(x[:, v : v + 1], (x.shape[0], LANES)) for v in range(count)], axis=0
    )


def pairs_kernel(
    live_ref, adj_ref, up_ref, down_ref, radial_ref, dist_ref, owner_ref, local_ref, analysis_ref,
    out_ref, ups_ref, m_ref, field_ref,
):
    comps, ves, points = adj_ref.shape
    fine = up_ref.shape[1]
    near = dist_ref.shape[0]
    pairs = near * ves
    groups = out_ref.shape[1]
    coefs = analysis_ref.shape[0]
    wide = coefs // groups
    high, low = split(analysis_ref[...])
    m = mm(high, down_ref[...]) + mm(low, down_ref[...])
    m_ref[...] = jnp.zeros_like(m_ref)
    for g in range(groups):
        m_ref[g * LANES : g * LANES + wide, :] = m[g * wide : (g + 1) * wide].astype(jnp.bfloat16)
    for c in range(comps):
        ups_ref[c] = mm(adj_ref[c], up_ref[...])
    owner = owner_ref[...]
    order = lax.broadcasted_iota(jnp.int32, owner.shape, 1) * near + lax.broadcasted_iota(
        jnp.int32, owner.shape, 0
    )
    dest = jnp.where(order < live_ref[0], owner // groups, -1)
    ident = (owner % groups) * ves + local_ref[...]
    lane = lax.broadcasted_iota(jnp.int32, (pairs, LANES), 1)
    hot = (columns(dest, ves) == lane).astype(jnp.float32)
    earlier = (
        lax.broadcasted_iota(jnp.int32, (pairs, pairs), 0)
        > lax.broadcasted_iota(jnp.int32, (pairs, pairs), 1)
    ).astype(jnp.float32)
    counts = mm(earlier.astype(jnp.bfloat16), hot.astype(jnp.bfloat16))
    ones = jnp.ones((8, LANES), jnp.bfloat16)
    rank = mm(ones, (hot * counts).astype(jnp.bfloat16), NT)
    place = mm(ones, (hot * (lane + 1).astype(jnp.float32)).astype(jnp.bfloat16), NT)
    slot = ((place - 1.0) * 12.0 + rank)[:1]
    row = lax.broadcasted_iota(jnp.int32, (32, 24, pairs), 1)
    base = lax.broadcasted_iota(jnp.int32, (32, 24, pairs), 0) * 12
    tile, inner = row // 8, row % 8
    code = (base + jnp.where(tile == 2, 8 + inner % 4, inner)).reshape(768, pairs)
    upper = jnp.where(tile == 2, inner // 4, tile).reshape(768, pairs)
    match = code == slot.astype(jnp.int32)
    pick_low = jnp.where(match & (upper == 0), 1.0, 0.0).astype(jnp.bfloat16)
    pick_high = jnp.where(match & (upper == 1), 1.0, 0.0).astype(jnp.bfloat16)
    dist = columns(dist_ref[...], ves)
    for start in range(0, fine, LANES):
        size = min(LANES, fine - start)
        at = slice(start, start + size)
        weight = 1.0 / (1.0 + dist[:, :size] * radial_ref[:, at])
        for c in range(comps):
            ups = jnp.concatenate(
                [jnp.broadcast_to(ups_ref[c, v : v + 1, at], (near, size)) for v in range(ves)], axis=0
            )
            field_ref[c, :, at] = (ups * weight).astype(jnp.bfloat16)
    part = [mm(field_ref[c], m_ref[...], NT) for c in range(comps)]
    ids = columns(ident.astype(jnp.float32), ves)
    for g in range(groups):
        at = slice(g * LANES, (g + 1) * LANES)
        second = pltpu.roll(part[1][:, at], wide, 1)
        third = pltpu.roll(part[2][:, at], 2 * wide - LANES, 1)
        low_half = jnp.where(lane < wide, part[0][:, at], second)
        high_half = jnp.where(lane < 2 * wide - LANES, second, third)
        high_half = jnp.where(lane == LANES - 1, ids, high_half)
        sent = mm(pick_low, low_half.astype(jnp.bfloat16)) + mm(
            pick_high, high_half.astype(jnp.bfloat16)
        )
        out_ref[:, g] = sent.reshape(32, 24, LANES).astype(jnp.bfloat16)


def self_kernel_body(adj_ref, jac_ref, kernel_ref, analysis_ref, out_ref):
    comps = adj_ref.shape[0]
    high, low = split(analysis_ref[...])
    s = mm(high, kernel_ref[...], NT) + mm(low, kernel_ref[...], NT)
    s_high, s_low = split(s)
    jac = jac_ref[...].astype(jnp.float32)
    for c in range(comps):
        scaled = (adj_ref[c].astype(jnp.float32) * jac).astype(jnp.bfloat16)
        out_ref[c] = mm(scaled, s_high, NT) + mm(scaled, s_low, NT)


def solve_kernel(group_ref, got_ref, self_ref, blocks_ref, out_ref):
    senders, rows, lanes = got_ref.shape
    comps, wide, ves = out_ref.shape
    got = got_ref[...].astype(jnp.float32)
    lane = lax.broadcasted_iota(jnp.int32, (senders, 8, lanes), 2).astype(jnp.float32)
    row = lax.broadcasted_iota(jnp.int32, (senders, 8, lanes), 1)
    first = got[:, 8:16, lanes - 1 : lanes] == lane
    other = jnp.where(got[:, 16:24, lanes - 1 : lanes] == lane, 1.0, 0.0)
    first = jnp.where(first, 1.0, 0.0)
    shifted = pltpu.roll(other, 4, 1)
    zero = jnp.zeros_like(first)
    to_low = jnp.concatenate([first, zero, jnp.where(row < 4, shifted, 0.0)], axis=1)
    to_high = jnp.concatenate([zero, first, jnp.where(row < 4, 0.0, other)], axis=1)
    flat = got_ref[...].reshape(senders * rows, lanes)
    near_low = mm(flat, to_low.reshape(senders * rows, lanes).astype(jnp.bfloat16), TN)
    near_high = mm(flat, to_high.reshape(senders * rows, lanes).astype(jnp.bfloat16), TN)
    cut = 2 * wide - lanes
    near = [
        near_low[:wide],
        jnp.concatenate([near_low[wide:], near_high[:cut]], axis=0),
        near_high[cut : cut + wide],
    ]
    rhs = [(self_ref[c] + near[c]).astype(jnp.bfloat16).astype(jnp.float32) for c in range(comps)]
    group = group_ref[0]
    at = lax.broadcasted_iota(jnp.int32, (wide, ves), 0)
    half = wide // 2

    def spread(r, c):
        b = [jnp.broadcast_to(blocks_ref[r, c, d : d + 1, :], (wide, ves)) for d in range(4)]
        lower = jnp.where(at < 4 * group + 3, b[0], b[1])
        upper = jnp.where(at < 4 * group + 5 + half, b[2], b[3])
        return jnp.where(at < half, lower, upper)

    m = [[spread(r, c) for c in range(3)] for r in range(3)]
    for c, value in enumerate(solve_three(m, rhs)):
        out_ref[c] = value


def solve_three(matrix, rhs):
    cofactor = [
        [
            matrix[1][1] * matrix[2][2] - matrix[1][2] * matrix[2][1],
            matrix[1][2] * matrix[2][0] - matrix[1][0] * matrix[2][2],
            matrix[1][0] * matrix[2][1] - matrix[1][1] * matrix[2][0],
        ],
        [
            matrix[0][2] * matrix[2][1] - matrix[0][1] * matrix[2][2],
            matrix[0][0] * matrix[2][2] - matrix[0][2] * matrix[2][0],
            matrix[0][1] * matrix[2][0] - matrix[0][0] * matrix[2][1],
        ],
        [
            matrix[0][1] * matrix[1][2] - matrix[0][2] * matrix[1][1],
            matrix[0][2] * matrix[1][0] - matrix[0][0] * matrix[1][2],
            matrix[0][0] * matrix[1][1] - matrix[0][1] * matrix[1][0],
        ],
    ]
    determinant = (
        matrix[0][0] * cofactor[0][0]
        + matrix[0][1] * cofactor[0][1]
        + matrix[0][2] * cofactor[0][2]
    )
    return [
        (cofactor[0][col] * rhs[0] + cofactor[1][col] * rhs[1] + cofactor[2][col] * rhs[2])
        / determinant
        for col in range(3)
    ]


def call_pairs(live, adj, up, down, radial, dist, owner, local, analysis, **kw):
    comps, ves, _ = adj.shape
    fine = up.shape[1]
    vmem = pl.BlockSpec(memory_space=pltpu.VMEM)
    return pl.pallas_call(
        pairs_kernel,
        out_shape=jax.ShapeDtypeStruct((32, 4, 24, LANES), jnp.bfloat16),
        in_specs=[pl.BlockSpec(memory_space=pltpu.SMEM)] + [vmem] * 8,
        out_specs=vmem,
        scratch_shapes=[
            pltpu.VMEM((comps, ves, fine), jnp.float32),
            pltpu.VMEM((4 * LANES, fine), jnp.bfloat16),
            pltpu.VMEM((comps, ves * dist.shape[0], fine), jnp.bfloat16),
        ],
        compiler_params=VMEM,
        name="pairs",
        **kw,
    )(live, adj, up, down, radial, dist, owner, local, analysis)


def call_self(adj, jac, kernel, analysis, **kw):
    comps, ves, _ = adj.shape
    return pl.pallas_call(
        self_kernel_body,
        out_shape=jax.ShapeDtypeStruct((comps, ves, analysis.shape[0]), jnp.float32),
        compiler_params=VMEM,
        name="self_term",
        **kw,
    )(adj, jac, kernel, analysis)


def call_solve(group, got, self_term, blocks, **kw):
    vmem = pl.BlockSpec(memory_space=pltpu.VMEM)
    return pl.pallas_call(
        solve_kernel,
        out_shape=jax.ShapeDtypeStruct(self_term.shape, jnp.float32),
        in_specs=[pl.BlockSpec(memory_space=pltpu.SMEM)] + [vmem] * 3,
        out_specs=vmem,
        compiler_params=VMEM,
        name="solve",
        **kw,
    )(group, got, self_term, blocks)


def body(
    adj_velocity,
    jacobian,
    self_kernel,
    near_kernel_up,
    near_kernel_down,
    radial,
    near_dist,
    near_owner,
    near_local,
    live_pairs,
    analysis,
    blocks,
):
    ves_dev, comps, points = adj_velocity.shape
    groups = lax.axis_size("deg")
    coefs = analysis.shape[1]
    wide = coefs // groups
    adj = adj_velocity.transpose(1, 0, 2)
    down = near_kernel_down.T
    projection = analysis.T
    sent = call_pairs(
        live_pairs, adj, near_kernel_up, down, radial[None, :], near_dist.T, near_owner.T,
        near_local.T, projection,
    )
    got = lax.all_to_all(
        sent.reshape(128, 24, LANES), ("ves", "deg"), split_axis=0, concat_axis=0, tiled=True
    )
    group = lax.axis_index("deg")
    own = call_self(adj, jacobian, self_kernel, projection)
    own = own.reshape(comps, ves_dev, groups, wide).transpose(2, 0, 3, 1)
    parts = [lax.dynamic_index_in_dim(own, group, 0, keepdims=False)]
    for i in range(1, groups):
        block = lax.dynamic_index_in_dim(own, (group + i) % groups, 0, keepdims=False)
        parts.append(lax.ppermute(block, "deg", [(j, (j + i) % groups) for j in range(groups)]))
    stacked = jnp.stack(parts)
    order = (group - jnp.arange(groups)) % groups
    self_term = jnp.take(stacked, order, axis=0).transpose(1, 2, 0, 3).reshape(comps, wide, -1)
    return call_solve(group[None].astype(jnp.int32), got, self_term, blocks.transpose(1, 2, 0, 3))


def solution(mesh):
    return jax.shard_map(
        body,
        mesh=mesh,
        in_specs=(
            P(("ves", "deg"), None, None),
            P(("ves", "deg"), None),
            P(),
            P(),
            P(),
            P(),
            P(("ves", "deg"), None),
            P(("ves", "deg"), None),
            P(("ves", "deg"), None),
            P(("ves", "deg")),
            P(),
            P("deg", None, None, "ves"),
        ),
        out_specs=P(None, "deg", "ves"),
        check_vma=False,
    )
```

```python
import jax
import jax.numpy as jnp
from jax import lax
from jax.experimental import pallas as pl
from jax.experimental.pallas import tpu as pltpu
from jax.sharding import PartitionSpec as P

LANES = 128
NN = (((1,), (0,)), ((), ()))
NT = (((1,), (1,)), ((), ()))
TN = (((0,), (0,)), ((), ()))
SLOTS = 12
ROWS = 2 * SLOTS


def mm(a, b, dims=NN):
    return lax.dot_general(a, b, dims, preferred_element_type=jnp.float32)


def split(x):
    high = x.astype(jnp.bfloat16)
    return high, (x - high.astype(jnp.float32)).astype(jnp.bfloat16)


def columns(x, count):
    return jnp.concatenate(
        [jnp.broadcast_to(x[:, v : v + 1], (x.shape[0], LANES)) for v in range(count)], axis=0
    )


def route(dest, ident, ves_count):
    near, ves = dest.shape
    pairs = near * ves
    lane = lax.broadcasted_iota(jnp.int32, (pairs, LANES), 1)
    hot = jnp.where(columns(dest, ves) == lane, 1.0, 0.0)
    earlier = jnp.where(
        lax.broadcasted_iota(jnp.int32, (pairs, pairs), 0)
        > lax.broadcasted_iota(jnp.int32, (pairs, pairs), 1),
        1.0,
        0.0,
    ).astype(jnp.bfloat16)
    counts = mm(earlier, hot.astype(jnp.bfloat16))
    ones = jnp.ones((8, LANES), jnp.bfloat16)
    rank = mm(ones, (hot * counts).astype(jnp.bfloat16), NT)
    place = mm(ones, (hot * (lane + 1).astype(jnp.float32)).astype(jnp.bfloat16), NT)
    ids = jnp.where(lane == 0, columns(ident.astype(jnp.float32), ves), 0.0)
    ids = mm(ones, ids.astype(jnp.bfloat16), NT)
    slot = ((place - 1.0) * SLOTS + rank)[:1].astype(jnp.int32)
    shape = (ves_count, ROWS, pairs)
    row = lax.broadcasted_iota(jnp.int32, shape, 1)
    base = lax.broadcasted_iota(jnp.int32, shape, 0) * SLOTS
    tile, inner = row // 8, row % 8
    code = (base + jnp.where(tile == 2, 8 + inner % 4, inner)).reshape(-1, pairs)
    upper = jnp.where(tile == 2, inner // 4, tile).reshape(-1, pairs)
    match = code == slot
    pick = [jnp.where(match & (upper == half), 1.0, 0.0) for half in range(2)]
    return jnp.concatenate(pick, axis=1).astype(jnp.bfloat16), ids


def pairs_kernel(
    live_ref, adj_hbm, up_hbm, down_hbm, radial_hbm, dist_hbm, owner_hbm, local_hbm, analysis_hbm,
    out_ref,
    adj_ref, up_ref, down_ref, radial_ref, dist_ref, owner_ref, local_ref, analysis_ref,
    ups_ref, field_ref, m_ref, sem,
):
    comps, ves, points = adj_ref.shape
    fine = up_ref.shape[1]
    near = dist_ref.shape[0]
    pairs = near * ves
    ves_count, groups = out_ref.shape[:2]
    wide = analysis_ref.shape[0] // groups
    half = fine // 2 // 256 * 256

    def fetch(i, source, target):
        copy = pltpu.make_async_copy(source, target, sem.at[i])
        copy.start()
        return copy

    small = [
        fetch(0, owner_hbm, owner_ref),
        fetch(1, local_hbm, local_ref),
        fetch(2, dist_hbm, dist_ref),
        fetch(3, radial_hbm, radial_ref.at[0]),
    ]
    get_analysis = fetch(4, analysis_hbm, analysis_ref)
    get_down = fetch(5, down_hbm.at[:, :half], down_ref.at[:, :half])
    get_rest = fetch(6, down_hbm.at[:, half:], down_ref.at[:, half:])
    get_adj = fetch(7, adj_hbm, adj_ref)
    get_up = fetch(8, up_hbm, up_ref)

    for copy in small:
        copy.wait()
    owner = owner_ref[...]
    order = lax.broadcasted_iota(jnp.int32, owner.shape, 1) * near + lax.broadcasted_iota(
        jnp.int32, owner.shape, 0
    )
    dest = jnp.where(order < live_ref[0], owner // groups, -1)
    pick, ids = route(dest, (owner % groups) * ves + local_ref[...], ves_count)
    dist = columns(dist_ref[...], ves)

    get_analysis.wait()
    high, low = split(analysis_ref[...])
    even = points // 256 * 256
    tails = jnp.concatenate([high[:, even:], low[:, even:]], axis=1)

    def project(start, stop):
        at = slice(start, stop)
        body = down_ref[:even, at]
        tail = down_ref[even:, at]
        m = mm(high[:, :even], body) + mm(low[:, :even], body)
        m_ref[:, at] = (m + mm(tails, jnp.concatenate([tail, tail], axis=0))).astype(jnp.bfloat16)

    def fields(start, stop):
        for s in range(start, stop, LANES):
            size = min(LANES, stop - s)
            at = slice(s, s + size)
            weight = 1.0 / (1.0 + dist[:, :size] * radial_ref[:, at])
            for c in range(comps):
                ups = [
                    jnp.broadcast_to(ups_ref[c * ves + v : c * ves + v + 1, at], (near, size))
                    for v in range(ves)
                ]
                value = jnp.concatenate(ups, axis=0) * weight
                field_ref[c * pairs : (c + 1) * pairs, at] = value.astype(jnp.bfloat16)

    get_down.wait()
    for s in range(0, half, 256):
        project(s, s + 256)
    get_adj.wait()
    get_up.wait()
    ups_ref[...] = mm(adj_ref[...].reshape(comps * ves, points), up_ref[...])
    get_rest.wait()
    for s in range(half, fine, 256):
        project(s, min(s + 256, fine))
        fields(s - half, min(s - half + 256, half))
        fields(s, min(s + 256, fine))
    part = mm(m_ref[...], field_ref[...], NT)

    zeros = jnp.zeros((2 * LANES - 3 * wide - 8, pairs), jnp.float32)

    def message(g):
        p = [part[g * wide : (g + 1) * wide, c * pairs : (c + 1) * pairs] for c in range(comps)]
        low_half = jnp.concatenate([p[0], p[1][: LANES - wide]], axis=0)
        high_half = jnp.concatenate([p[1][LANES - wide :], p[2], zeros, ids], axis=0)
        return jnp.concatenate([low_half, high_half], axis=1).astype(jnp.bfloat16)

    for g in range(0, groups, 2):
        sent = mm(pick, jnp.concatenate([message(g), message(g + 1)], axis=0), NT)
        for i in range(2):
            block = sent[:, i * LANES : (i + 1) * LANES]
            out_ref[:, g + i] = block.reshape(ves_count, ROWS, LANES).astype(jnp.bfloat16)


def call_pairs(ves_count, groups, live, adj, up, down, radial, dist, owner, local, analysis):
    comps, ves, _ = adj.shape
    fine = up.shape[1]
    pairs = ves * dist.shape[0]
    like = lambda a: pltpu.VMEM(a.shape, a.dtype)
    return pl.pallas_call(
        pairs_kernel,
        out_shape=jax.ShapeDtypeStruct((ves_count, groups, ROWS, LANES), jnp.bfloat16),
        in_specs=[pl.BlockSpec(memory_space=pltpu.SMEM)] + [pl.BlockSpec(memory_space=pl.ANY)] * 8,
        out_specs=pl.BlockSpec(memory_space=pltpu.VMEM),
        scratch_shapes=[
            like(adj), like(up), like(down), pltpu.VMEM((1, fine), jnp.float32),
            like(dist), like(owner), like(local), like(analysis),
            pltpu.VMEM((comps * ves, fine), jnp.float32),
            pltpu.VMEM((comps * pairs, fine), jnp.bfloat16),
            pltpu.VMEM((analysis.shape[0], fine), jnp.bfloat16),
            pltpu.SemaphoreType.DMA((9,)),
        ],
        compiler_params=pltpu.CompilerParams(vmem_limit_bytes=62 * 1024 * 1024),
        name="pairs",
    )(live, adj, up, down, radial, dist, owner, local, analysis)


def self_kernel_body(group_ref, adj_ref, jac_ref, kernel_ref, analysis_ref, *refs):
    *outs, s_ref = refs
    comps, ves, points = adj_ref.shape
    groups, wide, _ = s_ref.shape
    high, low = split(analysis_ref[...])
    s = mm(high, kernel_ref[...], NT) + mm(low, kernel_ref[...], NT)
    for g in range(groups):
        s_ref[g] = s[g * wide : (g + 1) * wide]
    scaled = (adj_ref[...].astype(jnp.float32) * jac_ref[...].astype(jnp.float32)[None]).astype(
        jnp.bfloat16
    )
    scaled = scaled.reshape(comps * ves, points)
    for i, out in enumerate(outs):
        s_high, s_low = split(s_ref[(group_ref[0] + i) % groups])
        value = mm(scaled, s_high, NT) + mm(scaled, s_low, NT)
        out[...] = jnp.concatenate(
            [value, jnp.zeros((comps * ves, LANES - wide), jnp.float32)], axis=1
        )


def call_self(groups, group, adj, jac, kernel, analysis):
    comps, ves, points = adj.shape
    vmem = pl.BlockSpec(memory_space=pltpu.VMEM)
    return pl.pallas_call(
        self_kernel_body,
        out_shape=[jax.ShapeDtypeStruct((comps * ves, LANES), jnp.float32)] * groups,
        in_specs=[pl.BlockSpec(memory_space=pltpu.SMEM)] + [vmem] * 4,
        out_specs=[vmem] * groups,
        scratch_shapes=[pltpu.VMEM((groups, analysis.shape[0] // groups, points), jnp.float32)],
        compiler_params=pltpu.CompilerParams(vmem_limit_bytes=16 * 1024 * 1024),
        name="self_term",
    )(group, adj, jac, kernel, analysis)


def solve_kernel(group_ref, got_ref, blocks_ref, *refs):
    *selfs, out_ref, self_ref = refs
    senders, rows, lanes = got_ref.shape
    comps, wide, ves = out_ref.shape
    groups = len(selfs)
    ves_dev = ves // groups
    group = group_ref[0]
    for i, ref in enumerate(selfs):
        self_ref[(group + groups - i) % groups] = ref[...]
    lane = lax.broadcasted_iota(jnp.int32, (senders, 8, lanes), 2).astype(jnp.float32)
    row = lax.broadcasted_iota(jnp.int32, (senders, 8, lanes), 1)
    first = got_ref[:, 8:16, lanes - 1 : lanes].astype(jnp.float32)
    other = got_ref[:, 16:24, lanes - 1 : lanes].astype(jnp.float32)
    first = jnp.where(first == lane, 1.0, 0.0)
    other = jnp.where(other == lane, 1.0, 0.0)
    zero = jnp.zeros_like(first)
    to_low = [first, zero, jnp.where(row < 4, pltpu.roll(other, 4, 1), 0.0)]
    to_high = [zero, first, jnp.where(row < 4, 0.0, other)]
    flat = got_ref[...].reshape(senders * rows, lanes)

    def gather(to):
        to = jnp.concatenate(to, axis=1).reshape(senders * rows, lanes).astype(jnp.bfloat16)
        return mm(flat, to, TN)

    near_low = gather(to_low)
    near_high = gather(to_high)
    cut = 2 * wide - lanes
    near = [
        near_low[:wide],
        jnp.concatenate([near_low[wide:], near_high[:cut]], axis=0),
        near_high[cut : cut + wide],
    ]
    rhs = []
    for c in range(comps):
        own = [self_ref[d, c * ves_dev : (c + 1) * ves_dev] for d in range(groups)]
        own = jnp.concatenate(own, axis=0).T[:wide]
        rhs.append((own + near[c]).astype(jnp.bfloat16).astype(jnp.float32))
    at = lax.broadcasted_iota(jnp.int32, (wide, ves), 0)
    half = wide // 2

    def spread(r, c):
        b = [jnp.broadcast_to(blocks_ref[r, c, d : d + 1, :], (wide, ves)) for d in range(4)]
        lower = jnp.where(at < 4 * group + 3, b[0], b[1])
        upper = jnp.where(at < 4 * group + 5 + half, b[2], b[3])
        return jnp.where(at < half, lower, upper)

    m = [[spread(r, c) for c in range(3)] for r in range(3)]
    for c, value in enumerate(solve_three(m, rhs)):
        out_ref[c] = value


def solve_three(matrix, rhs):
    cofactor = [
        [
            matrix[1][1] * matrix[2][2] - matrix[1][2] * matrix[2][1],
            matrix[1][2] * matrix[2][0] - matrix[1][0] * matrix[2][2],
            matrix[1][0] * matrix[2][1] - matrix[1][1] * matrix[2][0],
        ],
        [
            matrix[0][2] * matrix[2][1] - matrix[0][1] * matrix[2][2],
            matrix[0][0] * matrix[2][2] - matrix[0][2] * matrix[2][0],
            matrix[0][1] * matrix[2][0] - matrix[0][0] * matrix[2][1],
        ],
        [
            matrix[0][1] * matrix[1][2] - matrix[0][2] * matrix[1][1],
            matrix[0][2] * matrix[1][0] - matrix[0][0] * matrix[1][2],
            matrix[0][0] * matrix[1][1] - matrix[0][1] * matrix[1][0],
        ],
    ]
    determinant = (
        matrix[0][0] * cofactor[0][0]
        + matrix[0][1] * cofactor[0][1]
        + matrix[0][2] * cofactor[0][2]
    )
    return [
        (cofactor[0][col] * rhs[0] + cofactor[1][col] * rhs[1] + cofactor[2][col] * rhs[2])
        / determinant
        for col in range(3)
    ]


def call_solve(wide, group, got, blocks, selfs):
    comps = blocks.shape[0]
    ves = blocks.shape[-1]
    vmem = pl.BlockSpec(memory_space=pltpu.VMEM)
    return pl.pallas_call(
        solve_kernel,
        out_shape=jax.ShapeDtypeStruct((comps, wide, ves), jnp.float32),
        in_specs=[pl.BlockSpec(memory_space=pltpu.SMEM)] + [vmem] * (2 + len(selfs)),
        out_specs=vmem,
        scratch_shapes=[pltpu.VMEM((len(selfs),) + selfs[0].shape, jnp.float32)],
        compiler_params=pltpu.CompilerParams(vmem_limit_bytes=24 * 1024 * 1024),
        name="solve",
    )(group, got, blocks, *selfs)


def body(
    adj_velocity,
    jacobian,
    self_kernel,
    near_kernel_up,
    near_kernel_down,
    radial,
    near_dist,
    near_owner,
    near_local,
    live_pairs,
    analysis,
    blocks,
):
    ves_count, groups = lax.axis_size("ves"), lax.axis_size("deg")
    group = lax.axis_index("deg").astype(jnp.int32)[None]
    adj = adj_velocity.transpose(1, 0, 2)
    projection = analysis.T
    sent = call_pairs(
        ves_count, groups, live_pairs, adj, near_kernel_up, near_kernel_down.T, radial,
        near_dist.T, near_owner.T, near_local.T, projection,
    )
    sent, late = lax.optimization_barrier((sent, group))
    got = lax.all_to_all(
        sent.reshape(ves_count * groups, ROWS, LANES),
        ("ves", "deg"),
        split_axis=0,
        concat_axis=0,
        tiled=True,
    )
    selfs = call_self(groups, late, adj, jacobian, self_kernel, projection)
    selfs = [selfs[0]] + [
        lax.ppermute(selfs[i], "deg", [(j, (j + i) % groups) for j in range(groups)])
        for i in range(1, groups)
    ]
    return call_solve(
        analysis.shape[1] // groups, group, got, blocks.transpose(1, 2, 0, 3), selfs
    )


def solution(mesh):
    return jax.shard_map(
        body,
        mesh=mesh,
        in_specs=(
            P(("ves", "deg"), None, None),
            P(("ves", "deg"), None),
            P(),
            P(),
            P(),
            P(),
            P(("ves", "deg"), None),
            P(("ves", "deg"), None),
            P(("ves", "deg"), None),
            P(("ves", "deg")),
            P(),
            P("deg", None, None, "ves"),
        ),
        out_specs=P(None, "deg", "ves"),
        check_vma=False,
    )
```

```python
import jax
import jax.numpy as jnp
from jax import lax
from jax.experimental import pallas as pl
from jax.experimental.pallas import tpu as pltpu
from jax.sharding import PartitionSpec as P

LANES = 128
NN = (((1,), (0,)), ((), ()))
NT = (((1,), (1,)), ((), ()))
TN = (((0,), (0,)), ((), ()))
SLOTS = 12
ROWS = 2 * SLOTS


def mm(a, b, dims=NN):
    return lax.dot_general(a, b, dims, preferred_element_type=jnp.float32)


def split(x):
    high = x.astype(jnp.bfloat16)
    return high, (x - high.astype(jnp.float32)).astype(jnp.bfloat16)


def columns(x, count):
    return jnp.concatenate(
        [jnp.broadcast_to(x[:, v : v + 1], (x.shape[0], LANES)) for v in range(count)], axis=0
    )


def route(dest, ident, ves_count):
    near, ves = dest.shape
    pairs = near * ves
    lane = lax.broadcasted_iota(jnp.int32, (pairs, LANES), 1)
    hot = jnp.where(columns(dest, ves) == lane, 1.0, 0.0)
    earlier = jnp.where(
        lax.broadcasted_iota(jnp.int32, (pairs, pairs), 0)
        > lax.broadcasted_iota(jnp.int32, (pairs, pairs), 1),
        1.0,
        0.0,
    ).astype(jnp.bfloat16)
    counts = mm(earlier, hot.astype(jnp.bfloat16))
    ones = jnp.ones((8, LANES), jnp.bfloat16)
    rank = mm(ones, (hot * counts).astype(jnp.bfloat16), NT)
    place = mm(ones, (hot * (lane + 1).astype(jnp.float32)).astype(jnp.bfloat16), NT)
    ids = jnp.where(lane == 0, columns(ident.astype(jnp.float32), ves), 0.0)
    ids = mm(ones, ids.astype(jnp.bfloat16), NT)
    slot = ((place - 1.0) * SLOTS + rank)[:1].astype(jnp.int32)
    shape = (ves_count, ROWS, pairs)
    row = lax.broadcasted_iota(jnp.int32, shape, 1)
    base = lax.broadcasted_iota(jnp.int32, shape, 0) * SLOTS
    tile, inner = row // 8, row % 8
    code = (base + jnp.where(tile == 2, 8 + inner % 4, inner)).reshape(-1, pairs)
    upper = jnp.where(tile == 2, inner // 4, tile).reshape(-1, pairs)
    match = code == slot
    pick = [jnp.where(match & (upper == half), 1.0, 0.0) for half in range(2)]
    return jnp.concatenate(pick, axis=1).astype(jnp.bfloat16), ids


def pairs_kernel(
    live_hbm, adj_hbm, up_hbm, down_hbm, radial_hbm, dist_hbm, owner_hbm, local_hbm, analysis_hbm,
    out_hbm,
    live_ref, adj_ref, up_ref, down_ref, radial_ref, dist_ref, owner_ref, local_ref, analysis_ref,
    ups_ref, field_ref, m_ref, out_ref, sem,
):
    comps, ves, points = adj_ref.shape
    fine = up_ref.shape[1]
    near = dist_ref.shape[0]
    pairs = near * ves
    groups = out_ref.shape[0]
    ves_count = out_ref.shape[1] // ROWS
    wide = analysis_ref.shape[0] // groups
    half = fine // 2 // 256 * 256

    def fetch(i, source, target):
        copy = pltpu.make_async_copy(source, target, sem.at[i])
        copy.start()
        return copy

    small = [
        fetch(0, owner_hbm, owner_ref),
        fetch(1, local_hbm, local_ref),
        fetch(2, dist_hbm, dist_ref),
        fetch(3, radial_hbm, radial_ref.at[0]),
        fetch(10, live_hbm, live_ref),
    ]
    get_adj = fetch(4, adj_hbm, adj_ref)
    get_up = [fetch(5, up_hbm.at[:, :half], up_ref.at[:, :half])]
    get_analysis = fetch(6, analysis_hbm, analysis_ref)
    get_down = [fetch(7, down_hbm.at[:, :half], down_ref.at[:, :half])]
    for copy in small:
        copy.wait()
    get_up.append(fetch(8, up_hbm.at[:, half:], up_ref.at[:, half:]))
    get_down.append(fetch(9, down_hbm.at[:, half:], down_ref.at[:, half:]))

    owner = owner_ref[...]
    order = lax.broadcasted_iota(jnp.int32, owner.shape, 1) * near + lax.broadcasted_iota(
        jnp.int32, owner.shape, 0
    )
    dest = jnp.where(order < live_ref[0], owner // groups, -1)
    pick, ids = route(dest, (owner % groups) * ves + local_ref[...], ves_count)
    dist = columns(dist_ref[...], ves)
    get_adj.wait()
    adj = adj_ref[...].reshape(comps * ves, points)
    even = points // 256 * 256

    def project(start, stop):
        at = slice(start, stop)
        body = down_ref[:even, at]
        tail = down_ref[even:, at]
        m = mm(high[:, :even], body) + mm(low[:, :even], body)
        m_ref[:, at] = (m + mm(tails, jnp.concatenate([tail, tail], axis=0))).astype(jnp.bfloat16)

    def fields(start, stop):
        for s in range(start, stop, LANES):
            size = min(LANES, stop - s)
            at = slice(s, s + size)
            weight = 1.0 / (1.0 + dist[:, :size] * radial_ref[:, at])
            for c in range(comps):
                ups = [
                    jnp.broadcast_to(ups_ref[c * ves + v : c * ves + v + 1, at], (near, size))
                    for v in range(ves)
                ]
                value = jnp.concatenate(ups, axis=0) * weight
                field_ref[c * pairs : (c + 1) * pairs, at] = value.astype(jnp.bfloat16)

    for i, (start, stop) in enumerate([(0, half), (half, fine)]):
        get_up[i].wait()
        ups_ref[:, start:stop] = mm(adj, up_ref[:, start:stop])
        if i == 0:
            get_analysis.wait()
            high, low = split(analysis_ref[...])
            tails = jnp.concatenate([high[:, even:], low[:, even:]], axis=1)
        get_down[i].wait()
        for s in range(start, stop, 256):
            project(s, min(s + 256, stop))
            fields(s, min(s + 256, stop))
    part = mm(m_ref[...], field_ref[...], NT)

    zeros = jnp.zeros((2 * LANES - 3 * wide - 8, pairs), jnp.float32)

    def message(g):
        p = [part[g * wide : (g + 1) * wide, c * pairs : (c + 1) * pairs] for c in range(comps)]
        low_half = jnp.concatenate([p[0], p[1][: LANES - wide]], axis=0)
        high_half = jnp.concatenate([p[1][LANES - wide :], p[2], zeros, ids], axis=0)
        return jnp.concatenate([low_half, high_half], axis=1).astype(jnp.bfloat16)

    copies = []
    for g in range(0, groups, 2):
        sent = mm(pick, jnp.concatenate([message(g), message(g + 1)], axis=0), NT)
        for i in range(2):
            out_ref[g + i] = sent[:, i * LANES : (i + 1) * LANES].astype(jnp.bfloat16)
        copies.append(fetch(11 + g // 2, out_ref.at[g : g + 2], out_hbm.at[g : g + 2]))
    for copy in copies:
        copy.wait()


def call_pairs(ves_count, groups, live, adj, up, down, radial, dist, owner, local, analysis):
    comps, ves, _ = adj.shape
    fine = up.shape[1]
    pairs = ves * dist.shape[0]
    out = (groups, ves_count * ROWS, LANES)
    like = lambda a: pltpu.VMEM(a.shape, a.dtype)
    return pl.pallas_call(
        pairs_kernel,
        out_shape=jax.ShapeDtypeStruct(out, jnp.bfloat16),
        in_specs=[pl.BlockSpec(memory_space=pl.ANY)] * 9,
        out_specs=pl.BlockSpec(memory_space=pl.ANY),
        scratch_shapes=[
            pltpu.SMEM(live.shape, live.dtype), like(adj), like(up), like(down), pltpu.VMEM((1, fine), jnp.float32),
            like(dist), like(owner), like(local), like(analysis),
            pltpu.VMEM((comps * ves, fine), jnp.float32),
            pltpu.VMEM((comps * pairs, fine), jnp.bfloat16),
            pltpu.VMEM((analysis.shape[0], fine), jnp.bfloat16),
            pltpu.VMEM(out, jnp.bfloat16),
            pltpu.SemaphoreType.DMA((13,)),
        ],
        compiler_params=pltpu.CompilerParams(vmem_limit_bytes=61 * 1024 * 1024),
        name="pairs",
    )(live, adj, up, down, radial, dist, owner, local, analysis)


def self_kernel_body(group_ref, adj_ref, jac_ref, kernel_ref, analysis_ref, *refs):
    *outs, s_ref = refs
    comps, ves, points = adj_ref.shape
    groups, wide, _ = s_ref.shape
    high, low = split(analysis_ref[...])
    s = mm(high, kernel_ref[...], NT) + mm(low, kernel_ref[...], NT)
    for g in range(groups):
        s_ref[g] = s[g * wide : (g + 1) * wide]
    scaled = (adj_ref[...].astype(jnp.float32) * jac_ref[...].astype(jnp.float32)[None]).astype(
        jnp.bfloat16
    )
    scaled = scaled.reshape(comps * ves, points)
    for i, out in enumerate(outs):
        s_high, s_low = split(s_ref[(group_ref[0] + i) % groups])
        value = mm(scaled, s_high, NT) + mm(scaled, s_low, NT)
        out[...] = jnp.concatenate(
            [value, jnp.zeros((comps * ves, LANES - wide), jnp.float32)], axis=1
        )


def call_self(groups, group, adj, jac, kernel, analysis):
    comps, ves, points = adj.shape
    vmem = pl.BlockSpec(memory_space=pltpu.VMEM)
    return pl.pallas_call(
        self_kernel_body,
        out_shape=[jax.ShapeDtypeStruct((comps * ves, LANES), jnp.float32)] * groups,
        in_specs=[pl.BlockSpec(memory_space=pltpu.SMEM)] + [vmem] * 4,
        out_specs=[vmem] * groups,
        scratch_shapes=[pltpu.VMEM((groups, analysis.shape[0] // groups, points), jnp.float32)],
        compiler_params=pltpu.CompilerParams(vmem_limit_bytes=16 * 1024 * 1024),
        name="self_term",
    )(group, adj, jac, kernel, analysis)


def prepare_kernel(group_ref, blocks_ref, *refs):
    *selfs, self_ref, cofactor_ref, det_ref, order_ref = refs
    groups = len(selfs)
    comps, wide, ves = self_ref.shape
    ves_dev = ves // groups
    group = group_ref[0]
    for i, ref in enumerate(selfs):
        order_ref[(group + groups - i) % groups] = ref[...]
    for c in range(comps):
        own = [order_ref[d, c * ves_dev : (c + 1) * ves_dev] for d in range(groups)]
        self_ref[c] = jnp.concatenate(own, axis=0).T[:wide]
    at = lax.broadcasted_iota(jnp.int32, (wide, ves), 0)
    half = wide // 2

    def spread(r, c):
        b = [jnp.broadcast_to(blocks_ref[r, c, d : d + 1, :], (wide, ves)) for d in range(4)]
        lower = jnp.where(at < 4 * group + 3, b[0], b[1])
        upper = jnp.where(at < 4 * group + 5 + half, b[2], b[3])
        return jnp.where(at < half, lower, upper)

    m = [[spread(r, c) for c in range(3)] for r in range(3)]

    def cofactor(r, c):
        r1, r2, c1, c2 = (r + 1) % 3, (r + 2) % 3, (c + 1) % 3, (c + 2) % 3
        return m[r1][c1] * m[r2][c2] - m[r1][c2] * m[r2][c1]

    first = [cofactor(0, c) for c in range(3)]
    det_ref[...] = m[0][0] * first[0] + m[0][1] * first[1] + m[0][2] * first[2]
    for r in range(3):
        for c in range(3):
            cofactor_ref[r, c] = first[c] if r == 0 else cofactor(r, c)


def call_prepare(wide, group, blocks, selfs):
    comps, ves = blocks.shape[0], blocks.shape[-1]
    vmem = pl.BlockSpec(memory_space=pltpu.VMEM)
    f32 = jnp.float32
    return pl.pallas_call(
        prepare_kernel,
        out_shape=[
            pltpu.VMEM((comps, wide, ves), f32),
            pltpu.VMEM((3, 3, wide, ves), f32),
            pltpu.VMEM((wide, ves), f32),
        ],
        in_specs=[pl.BlockSpec(memory_space=pltpu.SMEM)] + [vmem] * (1 + len(selfs)),
        out_specs=[vmem] * 3,
        scratch_shapes=[pltpu.VMEM((len(selfs),) + selfs[0].shape, f32)],
        compiler_params=pltpu.CompilerParams(vmem_limit_bytes=16 * 1024 * 1024),
        name="prepare",
    )(group, blocks, *selfs)


def solve_kernel(got_ref, self_ref, cofactor_ref, det_ref, out_ref):
    senders, rows, lanes = got_ref.shape
    comps, wide, ves = out_ref.shape
    lane = lax.broadcasted_iota(jnp.int32, (senders, 8, lanes), 2).astype(jnp.float32)
    row = lax.broadcasted_iota(jnp.int32, (senders, 8, lanes), 1)
    first = got_ref[:, 8:16, lanes - 1 : lanes].astype(jnp.float32)
    other = got_ref[:, 16:24, lanes - 1 : lanes].astype(jnp.float32)
    first = jnp.where(first == lane, 1.0, 0.0)
    other = jnp.where(other == lane, 1.0, 0.0)
    zero = jnp.zeros_like(first)
    to_low = [first, zero, jnp.where(row < 4, pltpu.roll(other, 4, 1), 0.0)]
    to_high = [zero, first, jnp.where(row < 4, 0.0, other)]
    flat = got_ref[...].reshape(senders * rows, lanes)

    to = [jnp.concatenate(t, axis=1).reshape(senders * rows, lanes) for t in (to_low, to_high)]
    both = mm(flat, jnp.concatenate(to, axis=1).astype(jnp.bfloat16), TN)
    near_low, near_high = both[:, :lanes], both[:, lanes:]
    cut = 2 * wide - lanes
    near = [
        near_low[:wide],
        jnp.concatenate([near_low[wide:], near_high[:cut]], axis=0),
        near_high[cut : cut + wide],
    ]
    rhs = [(self_ref[c] + near[c]).astype(jnp.bfloat16).astype(jnp.float32) for c in range(comps)]
    det = det_ref[...]
    for c in range(comps):
        out_ref[c] = (
            cofactor_ref[0, c] * rhs[0] + cofactor_ref[1, c] * rhs[1] + cofactor_ref[2, c] * rhs[2]
        ) / det


def call_solve(got, prepared):
    vmem = pl.BlockSpec(memory_space=pltpu.VMEM)
    return pl.pallas_call(
        solve_kernel,
        out_shape=jax.ShapeDtypeStruct(prepared[0].shape, jnp.float32),
        in_specs=[vmem] * (1 + len(prepared)),
        out_specs=vmem,
        compiler_params=pltpu.CompilerParams(vmem_limit_bytes=24 * 1024 * 1024),
        name="solve",
    )(got, *prepared)


def body(
    adj_velocity,
    jacobian,
    self_kernel,
    near_kernel_up,
    near_kernel_down,
    radial,
    near_dist,
    near_owner,
    near_local,
    live_pairs,
    analysis,
    blocks,
):
    ves_count, groups = lax.axis_size("ves"), lax.axis_size("deg")
    group = lax.axis_index("deg").astype(jnp.int32)[None]
    adj = adj_velocity.transpose(1, 0, 2)
    projection = analysis.T
    sent = call_pairs(
        ves_count, groups, live_pairs, adj, near_kernel_up, near_kernel_down.T, radial,
        near_dist.T, near_owner.T, near_local.T, projection,
    )
    sent, late = lax.optimization_barrier((sent, group))
    got = lax.all_to_all(
        sent.reshape(groups * ves_count, ROWS, LANES),
        ("deg", "ves"),
        split_axis=0,
        concat_axis=0,
        tiled=True,
    )
    selfs = call_self(groups, late, adj, jacobian, self_kernel, projection)
    selfs = [selfs[0]] + [
        lax.ppermute(selfs[i], "deg", [(j, (j + i) % groups) for j in range(groups)])
        for i in range(1, groups)
    ]
    wide = analysis.shape[1] // groups
    prepared = call_prepare(wide, group, blocks.transpose(1, 2, 0, 3), selfs)
    return call_solve(got, prepared)


def solution(mesh):
    return jax.shard_map(
        body,
        mesh=mesh,
        in_specs=(
            P(("ves", "deg"), None, None),
            P(("ves", "deg"), None),
            P(),
            P(),
            P(),
            P(),
            P(("ves", "deg"), None),
            P(("ves", "deg"), None),
            P(("ves", "deg"), None),
            P(("ves", "deg")),
            P(),
            P("deg", None, None, "ves"),
        ),
        out_specs=P(None, "deg", "ves"),
        check_vma=False,
    )
```

```python
import jax
import jax.numpy as jnp
from jax import lax
from jax.experimental import pallas as pl
from jax.experimental.pallas import tpu as pltpu
from jax.sharding import PartitionSpec as P

LANES = 128
NN = (((1,), (0,)), ((), ()))
NT = (((1,), (1,)), ((), ()))
TN = (((0,), (0,)), ((), ()))
SLOTS = 12
ROWS = 2 * SLOTS


def mm(a, b, dims=NN):
    return lax.dot_general(a, b, dims, preferred_element_type=jnp.float32)


def split(x):
    high = x.astype(jnp.bfloat16)
    return high, (x - high.astype(jnp.float32)).astype(jnp.bfloat16)


def columns(x, count):
    return jnp.concatenate(
        [jnp.broadcast_to(x[:, v : v + 1], (x.shape[0], LANES)) for v in range(count)], axis=0
    )


def route(dest, ident, ves_count):
    near, ves = dest.shape
    pairs = near * ves
    lane = lax.broadcasted_iota(jnp.int32, (pairs, LANES), 1)
    hot = jnp.where(columns(dest, ves) == lane, 1.0, 0.0)
    earlier = jnp.where(
        lax.broadcasted_iota(jnp.int32, (pairs, pairs), 0)
        > lax.broadcasted_iota(jnp.int32, (pairs, pairs), 1),
        1.0,
        0.0,
    ).astype(jnp.bfloat16)
    counts = mm(earlier, hot.astype(jnp.bfloat16))
    ones = jnp.ones((8, LANES), jnp.bfloat16)
    rank = mm(ones, (hot * counts).astype(jnp.bfloat16), NT)
    place = mm(ones, (hot * (lane + 1).astype(jnp.float32)).astype(jnp.bfloat16), NT)
    ids = jnp.where(lane == 0, columns(ident.astype(jnp.float32), ves), 0.0)
    ids = mm(ones, ids.astype(jnp.bfloat16), NT)
    slot = ((place - 1.0) * SLOTS + rank)[:1].astype(jnp.int32)
    shape = (ves_count, ROWS, pairs)
    row = lax.broadcasted_iota(jnp.int32, shape, 1)
    base = lax.broadcasted_iota(jnp.int32, shape, 0) * SLOTS
    tile, inner = row // 8, row % 8
    code = (base + jnp.where(tile == 2, 8 + inner % 4, inner)).reshape(-1, pairs)
    upper = jnp.where(tile == 2, inner // 4, tile).reshape(-1, pairs)
    match = code == slot
    pick = [jnp.where(match & (upper == half), 1.0, 0.0) for half in range(2)]
    return jnp.concatenate(pick, axis=1).astype(jnp.bfloat16), ids


def pairs_kernel(
    live_hbm, adj_hbm, up_hbm, down_hbm, radial_hbm, dist_hbm, owner_hbm, local_hbm, analysis_hbm,
    out_hbm,
    live_ref, adj_ref, up_ref, down_ref, radial_ref, dist_ref, owner_ref, local_ref, analysis_ref,
    ups_ref, field_ref, m_ref, out_ref, sem,
):
    comps, ves, points = adj_ref.shape
    fine = up_ref.shape[1]
    near = dist_ref.shape[0]
    pairs = near * ves
    groups = out_ref.shape[0]
    ves_count = out_ref.shape[1] // ROWS
    wide = analysis_ref.shape[0] // groups
    half = fine // 2 // 256 * 256

    def fetch(i, source, target):
        copy = pltpu.make_async_copy(source, target, sem.at[i])
        copy.start()
        return copy

    small = [
        fetch(0, owner_hbm, owner_ref),
        fetch(1, local_hbm, local_ref),
        fetch(2, dist_hbm, dist_ref),
        fetch(3, radial_hbm, radial_ref.at[0]),
        fetch(10, live_hbm, live_ref),
    ]
    get_adj = fetch(4, adj_hbm, adj_ref)
    get_up = [fetch(5, up_hbm.at[:, :half], up_ref.at[:, :half])]
    get_analysis = fetch(6, analysis_hbm, analysis_ref)
    get_down = [fetch(7, down_hbm.at[:, :half], down_ref.at[:, :half])]
    for copy in small:
        copy.wait()
    get_up.append(fetch(8, up_hbm.at[:, half:], up_ref.at[:, half:]))
    get_down.append(fetch(9, down_hbm.at[:, half:], down_ref.at[:, half:]))

    owner = owner_ref[...]
    order = lax.broadcasted_iota(jnp.int32, owner.shape, 1) * near + lax.broadcasted_iota(
        jnp.int32, owner.shape, 0
    )
    dest = jnp.where(order < live_ref[0], owner // groups, -1)
    pick, ids = route(dest, (owner % groups) * ves + local_ref[...], ves_count)
    dist = columns(dist_ref[...], ves)
    get_adj.wait()
    adj = adj_ref[...].reshape(comps * ves, points)
    even = points // 256 * 256
    refined = 256 - (points - even)

    def project(start, stop):
        at = slice(start, stop)
        last = jnp.concatenate([down_ref[even:, at], down_ref[:refined, at]], axis=0)
        m_ref[:, at] = (mm(high[:, :even], down_ref[:even, at]) + mm(tails, last)).astype(jnp.bfloat16)

    def fields(start, stop):
        for s in range(start, stop, LANES):
            size = min(LANES, stop - s)
            at = slice(s, s + size)
            weight = 1.0 / (1.0 + dist[:, :size] * radial_ref[:, at])
            for c in range(comps):
                ups = [
                    jnp.broadcast_to(ups_ref[c * ves + v : c * ves + v + 1, at], (near, size))
                    for v in range(ves)
                ]
                value = jnp.concatenate(ups, axis=0) * weight
                field_ref[c * pairs : (c + 1) * pairs, at] = value.astype(jnp.bfloat16)

    for i, (start, stop) in enumerate([(0, half), (half, fine)]):
        get_up[i].wait()
        ups_ref[:, start:stop] = mm(adj, up_ref[:, start:stop])
        if i == 0:
            get_analysis.wait()
            high, low = split(analysis_ref[...])
            tails = jnp.concatenate([high[:, even:], low[:, :refined]], axis=1)
        get_down[i].wait()
        for s in range(start, stop, 256):
            project(s, min(s + 256, stop))
            fields(s, min(s + 256, stop))
    part = mm(m_ref[...], field_ref[...], NT)

    zeros = jnp.zeros((2 * LANES - 3 * wide - 8, pairs), jnp.float32)

    def message(g):
        p = [part[g * wide : (g + 1) * wide, c * pairs : (c + 1) * pairs] for c in range(comps)]
        low_half = jnp.concatenate([p[0], p[1][: LANES - wide]], axis=0)
        high_half = jnp.concatenate([p[1][LANES - wide :], p[2], zeros, ids], axis=0)
        return jnp.concatenate([low_half, high_half], axis=1).astype(jnp.bfloat16)

    copies = []
    for g in range(0, groups, 2):
        sent = mm(pick, jnp.concatenate([message(g), message(g + 1)], axis=0), NT)
        for i in range(2):
            out_ref[g + i] = sent[:, i * LANES : (i + 1) * LANES].astype(jnp.bfloat16)
        copies.append(fetch(11 + g // 2, out_ref.at[g : g + 2], out_hbm.at[g : g + 2]))
    for copy in copies:
        copy.wait()


def call_pairs(ves_count, groups, live, adj, up, down, radial, dist, owner, local, analysis):
    comps, ves, _ = adj.shape
    fine = up.shape[1]
    pairs = ves * dist.shape[0]
    out = (groups, ves_count * ROWS, LANES)
    like = lambda a: pltpu.VMEM(a.shape, a.dtype)
    return pl.pallas_call(
        pairs_kernel,
        out_shape=jax.ShapeDtypeStruct(out, jnp.bfloat16),
        in_specs=[pl.BlockSpec(memory_space=pl.ANY)] * 9,
        out_specs=pl.BlockSpec(memory_space=pl.ANY),
        scratch_shapes=[
            pltpu.SMEM(live.shape, live.dtype), like(adj), like(up), like(down), pltpu.VMEM((1, fine), jnp.float32),
            like(dist), like(owner), like(local), like(analysis),
            pltpu.VMEM((comps * ves, fine), jnp.float32),
            pltpu.VMEM((comps * pairs, fine), jnp.bfloat16),
            pltpu.VMEM((analysis.shape[0], fine), jnp.bfloat16),
            pltpu.VMEM(out, jnp.bfloat16),
            pltpu.SemaphoreType.DMA((13,)),
        ],
        compiler_params=pltpu.CompilerParams(vmem_limit_bytes=61 * 1024 * 1024),
        name="pairs",
    )(live, adj, up, down, radial, dist, owner, local, analysis)


def self_kernel_body(group_ref, adj_ref, jac_ref, kernel_ref, analysis_ref, *refs):
    *outs, s_ref = refs
    comps, ves, points = adj_ref.shape
    groups, wide, _ = s_ref.shape
    high, low = split(analysis_ref[...])
    s = mm(high, kernel_ref[...], NT) + mm(low, kernel_ref[...], NT)
    for g in range(groups):
        s_ref[g] = s[g * wide : (g + 1) * wide]
    scaled = (adj_ref[...].astype(jnp.float32) * jac_ref[...].astype(jnp.float32)[None]).astype(
        jnp.bfloat16
    )
    scaled = scaled.reshape(comps * ves, points)
    for i, out in enumerate(outs):
        s_high, s_low = split(s_ref[(group_ref[0] + i) % groups])
        value = mm(scaled, s_high, NT) + mm(scaled, s_low, NT)
        out[...] = jnp.concatenate(
            [value, jnp.zeros((comps * ves, LANES - wide), jnp.float32)], axis=1
        )


def call_self(groups, group, adj, jac, kernel, analysis):
    comps, ves, points = adj.shape
    vmem = pl.BlockSpec(memory_space=pltpu.VMEM)
    return pl.pallas_call(
        self_kernel_body,
        out_shape=[jax.ShapeDtypeStruct((comps * ves, LANES), jnp.float32)] * groups,
        in_specs=[pl.BlockSpec(memory_space=pltpu.SMEM)] + [vmem] * 4,
        out_specs=[vmem] * groups,
        scratch_shapes=[pltpu.VMEM((groups, analysis.shape[0] // groups, points), jnp.float32)],
        compiler_params=pltpu.CompilerParams(vmem_limit_bytes=16 * 1024 * 1024),
        name="self_term",
    )(group, adj, jac, kernel, analysis)


def prepare_kernel(group_ref, blocks_ref, *refs):
    *selfs, self_ref, cofactor_ref, det_ref, order_ref = refs
    groups = len(selfs)
    comps, wide, ves = self_ref.shape
    ves_dev = ves // groups
    group = group_ref[0]
    for i, ref in enumerate(selfs):
        order_ref[(group + groups - i) % groups] = ref[...]
    for c in range(comps):
        own = [order_ref[d, c * ves_dev : (c + 1) * ves_dev] for d in range(groups)]
        self_ref[c] = jnp.concatenate(own, axis=0).T[:wide]
    at = lax.broadcasted_iota(jnp.int32, (wide, ves), 0)
    half = wide // 2

    def spread(r, c):
        b = [jnp.broadcast_to(blocks_ref[r, c, d : d + 1, :], (wide, ves)) for d in range(4)]
        lower = jnp.where(at < 4 * group + 3, b[0], b[1])
        upper = jnp.where(at < 4 * group + 5 + half, b[2], b[3])
        return jnp.where(at < half, lower, upper)

    m = [[spread(r, c) for c in range(3)] for r in range(3)]

    def cofactor(r, c):
        r1, r2, c1, c2 = (r + 1) % 3, (r + 2) % 3, (c + 1) % 3, (c + 2) % 3
        return m[r1][c1] * m[r2][c2] - m[r1][c2] * m[r2][c1]

    first = [cofactor(0, c) for c in range(3)]
    det_ref[...] = m[0][0] * first[0] + m[0][1] * first[1] + m[0][2] * first[2]
    for r in range(3):
        for c in range(3):
            cofactor_ref[r, c] = first[c] if r == 0 else cofactor(r, c)


def call_prepare(wide, group, blocks, selfs):
    comps, ves = blocks.shape[0], blocks.shape[-1]
    vmem = pl.BlockSpec(memory_space=pltpu.VMEM)
    f32 = jnp.float32
    return pl.pallas_call(
        prepare_kernel,
        out_shape=[
            pltpu.VMEM((comps, wide, ves), f32),
            pltpu.VMEM((3, 3, wide, ves), f32),
            pltpu.VMEM((wide, ves), f32),
        ],
        in_specs=[pl.BlockSpec(memory_space=pltpu.SMEM)] + [vmem] * (1 + len(selfs)),
        out_specs=[vmem] * 3,
        scratch_shapes=[pltpu.VMEM((len(selfs),) + selfs[0].shape, f32)],
        compiler_params=pltpu.CompilerParams(vmem_limit_bytes=16 * 1024 * 1024),
        name="prepare",
    )(group, blocks, *selfs)


def solve_kernel(got_ref, self_ref, cofactor_ref, det_ref, out_ref):
    senders, rows, lanes = got_ref.shape
    comps, wide, ves = out_ref.shape
    lane = lax.broadcasted_iota(jnp.int32, (senders, 8, lanes), 2).astype(jnp.float32)
    row = lax.broadcasted_iota(jnp.int32, (senders, 8, lanes), 1)
    first = got_ref[:, 8:16, lanes - 1 : lanes].astype(jnp.float32)
    other = got_ref[:, 16:24, lanes - 1 : lanes].astype(jnp.float32)
    first = jnp.where(first == lane, 1.0, 0.0)
    other = jnp.where(other == lane, 1.0, 0.0)
    zero = jnp.zeros_like(first)
    to_low = [first, zero, jnp.where(row < 4, pltpu.roll(other, 4, 1), 0.0)]
    to_high = [zero, first, jnp.where(row < 4, 0.0, other)]
    flat = got_ref[...].reshape(senders * rows, lanes)

    to = [jnp.concatenate(t, axis=1).reshape(senders * rows, lanes) for t in (to_low, to_high)]
    both = mm(flat, jnp.concatenate(to, axis=1).astype(jnp.bfloat16), TN)
    near_low, near_high = both[:, :lanes], both[:, lanes:]
    cut = 2 * wide - lanes
    near = [
        near_low[:wide],
        jnp.concatenate([near_low[wide:], near_high[:cut]], axis=0),
        near_high[cut : cut + wide],
    ]
    rhs = [(self_ref[c] + near[c]).astype(jnp.bfloat16).astype(jnp.float32) for c in range(comps)]
    det = det_ref[...]
    for c in range(comps):
        out_ref[c] = (
            cofactor_ref[0, c] * rhs[0] + cofactor_ref[1, c] * rhs[1] + cofactor_ref[2, c] * rhs[2]
        ) / det


def call_solve(got, prepared):
    vmem = pl.BlockSpec(memory_space=pltpu.VMEM)
    return pl.pallas_call(
        solve_kernel,
        out_shape=jax.ShapeDtypeStruct(prepared[0].shape, jnp.float32),
        in_specs=[vmem] * (1 + len(prepared)),
        out_specs=vmem,
        compiler_params=pltpu.CompilerParams(vmem_limit_bytes=24 * 1024 * 1024),
        name="solve",
    )(got, *prepared)


def body(
    adj_velocity,
    jacobian,
    self_kernel,
    near_kernel_up,
    near_kernel_down,
    radial,
    near_dist,
    near_owner,
    near_local,
    live_pairs,
    analysis,
    blocks,
):
    ves_count, groups = lax.axis_size("ves"), lax.axis_size("deg")
    group = lax.axis_index("deg").astype(jnp.int32)[None]
    adj = adj_velocity.transpose(1, 0, 2)
    projection = analysis.T
    sent = call_pairs(
        ves_count, groups, live_pairs, adj, near_kernel_up, near_kernel_down.T, radial,
        near_dist.T, near_owner.T, near_local.T, projection,
    )
    sent, late = lax.optimization_barrier((sent, group))
    got = lax.all_to_all(
        sent.reshape(groups * ves_count, ROWS, LANES),
        ("deg", "ves"),
        split_axis=0,
        concat_axis=0,
        tiled=True,
    )
    selfs = call_self(groups, late, adj, jacobian, self_kernel, projection)
    selfs = [selfs[0]] + [
        lax.ppermute(selfs[i], "deg", [(j, (j + i) % groups) for j in range(groups)])
        for i in range(1, groups)
    ]
    wide = analysis.shape[1] // groups
    prepared = call_prepare(wide, group, blocks.transpose(1, 2, 0, 3), selfs)
    return call_solve(got, prepared)


def solution(mesh):
    return jax.shard_map(
        body,
        mesh=mesh,
        in_specs=(
            P(("ves", "deg"), None, None),
            P(("ves", "deg"), None),
            P(),
            P(),
            P(),
            P(),
            P(("ves", "deg"), None),
            P(("ves", "deg"), None),
            P(("ves", "deg"), None),
            P(("ves", "deg")),
            P(),
            P("deg", None, None, "ves"),
        ),
        out_specs=P(None, "deg", "ves"),
        check_vma=False,
    )
```

```python
import jax
import jax.numpy as jnp
from jax import lax
from jax.experimental import pallas as pl
from jax.experimental.pallas import tpu as pltpu
from jax.sharding import PartitionSpec as P

LANES = 128
NN = (((1,), (0,)), ((), ()))
NT = (((1,), (1,)), ((), ()))
TN = (((0,), (0,)), ((), ()))
SLOTS = 12
ROWS = 2 * SLOTS


def mm(a, b, dims=NN):
    return lax.dot_general(a, b, dims, preferred_element_type=jnp.float32)


def split(x):
    high = x.astype(jnp.bfloat16)
    return high, (x - high.astype(jnp.float32)).astype(jnp.bfloat16)


def columns(x, count):
    return jnp.concatenate(
        [jnp.broadcast_to(x[:, v : v + 1], (x.shape[0], LANES)) for v in range(count)], axis=0
    )


def route(dest, ident, ves_count):
    near, ves = dest.shape
    pairs = near * ves
    lane = lax.broadcasted_iota(jnp.int32, (pairs, LANES), 1)
    hot = jnp.where(columns(dest, ves) == lane, 1.0, 0.0)
    earlier = jnp.where(
        lax.broadcasted_iota(jnp.int32, (pairs, pairs), 0)
        > lax.broadcasted_iota(jnp.int32, (pairs, pairs), 1),
        1.0,
        0.0,
    ).astype(jnp.bfloat16)
    counts = mm(earlier, hot.astype(jnp.bfloat16))
    ones = jnp.ones((8, LANES), jnp.bfloat16)
    rank = mm(ones, (hot * counts).astype(jnp.bfloat16), NT)
    place = mm(ones, (hot * (lane + 1).astype(jnp.float32)).astype(jnp.bfloat16), NT)
    ids = jnp.where(lane == 0, columns(ident.astype(jnp.float32), ves), 0.0)
    ids = mm(ones, ids.astype(jnp.bfloat16), NT)
    slot = ((place - 1.0) * SLOTS + rank)[:1].astype(jnp.int32)
    shape = (ves_count, ROWS, pairs)
    row = lax.broadcasted_iota(jnp.int32, shape, 1)
    base = lax.broadcasted_iota(jnp.int32, shape, 0) * SLOTS
    tile, inner = row // 8, row % 8
    code = (base + jnp.where(tile == 2, 8 + inner % 4, inner)).reshape(-1, pairs)
    upper = jnp.where(tile == 2, inner // 4, tile).reshape(-1, pairs)
    match = code == slot
    pick = [jnp.where(match & (upper == half), 1.0, 0.0) for half in range(2)]
    return jnp.concatenate(pick, axis=1).astype(jnp.bfloat16), ids


def pairs_kernel(
    live_hbm, adj_hbm, up_hbm, down_hbm, radial_hbm, dist_hbm, owner_hbm, local_hbm, analysis_hbm,
    out_hbm,
    live_ref, adj_ref, up_ref, down_ref, radial_ref, dist_ref, owner_ref, local_ref, analysis_ref,
    ups_ref, field_ref, m_ref, out_ref, sem,
):
    comps, ves, points = adj_ref.shape
    fine = up_ref.shape[1]
    near = dist_ref.shape[0]
    pairs = near * ves
    groups = out_ref.shape[0]
    ves_count = out_ref.shape[1] // ROWS
    wide = analysis_ref.shape[0] // groups
    half = fine // 2 // 256 * 256

    def fetch(i, source, target):
        copy = pltpu.make_async_copy(source, target, sem.at[i])
        copy.start()
        return copy

    small = [
        fetch(0, owner_hbm, owner_ref),
        fetch(1, local_hbm, local_ref),
        fetch(2, dist_hbm, dist_ref),
        fetch(3, radial_hbm, radial_ref.at[0]),
        fetch(10, live_hbm, live_ref),
    ]
    get_adj = fetch(4, adj_hbm, adj_ref)
    get_up = [fetch(5, up_hbm.at[:, :half], up_ref.at[:, :half])]
    get_analysis = fetch(6, analysis_hbm, analysis_ref)
    get_down = [fetch(7, down_hbm.at[:, :half], down_ref.at[:, :half])]
    for copy in small:
        copy.wait()
    get_up.append(fetch(8, up_hbm.at[:, half:], up_ref.at[:, half:]))
    get_down.append(fetch(9, down_hbm.at[:, half:], down_ref.at[:, half:]))

    owner = owner_ref[...]
    order = lax.broadcasted_iota(jnp.int32, owner.shape, 1) * near + lax.broadcasted_iota(
        jnp.int32, owner.shape, 0
    )
    dest = jnp.where(order < live_ref[0], owner // groups, -1)
    pick, ids = route(dest, (owner % groups) * ves + local_ref[...], ves_count)
    dist = columns(dist_ref[...], ves)
    get_adj.wait()
    adj = adj_ref[...].reshape(comps * ves, points)
    even = points // 256 * 256
    refined = 256 - (points - even)

    def project(start, stop):
        at = slice(start, stop)
        last = jnp.concatenate([down_ref[even:, at], down_ref[:refined, at]], axis=0)
        m_ref[:, at] = (mm(high[:, :even], down_ref[:even, at]) + mm(tails, last)).astype(jnp.bfloat16)

    def fields(start, stop):
        for s in range(start, stop, LANES):
            size = min(LANES, stop - s)
            at = slice(s, s + size)
            weight = 1.0 / (1.0 + dist[:, :size] * radial_ref[:, at])
            for c in range(comps):
                ups = [
                    jnp.broadcast_to(ups_ref[c * ves + v : c * ves + v + 1, at], (near, size))
                    for v in range(ves)
                ]
                value = jnp.concatenate(ups, axis=0) * weight
                field_ref[c * pairs : (c + 1) * pairs, at] = value.astype(jnp.bfloat16)

    for i, (start, stop) in enumerate([(0, half), (half, fine)]):
        get_up[i].wait()
        ups_ref[:, start:stop] = mm(adj, up_ref[:, start:stop])
        if i == 0:
            get_analysis.wait()
            high, low = split(analysis_ref[...])
            tails = jnp.concatenate([high[:, even:], low[:, :refined]], axis=1)
        get_down[i].wait()
        for s in range(start, stop, 256):
            project(s, min(s + 256, stop))
            fields(s, min(s + 256, stop))
    part = mm(m_ref[...], field_ref[...], NT)

    zeros = jnp.zeros((2 * LANES - 3 * wide - 8, pairs), jnp.float32)

    def message(g):
        p = [part[g * wide : (g + 1) * wide, c * pairs : (c + 1) * pairs] for c in range(comps)]
        low_half = jnp.concatenate([p[0], p[1][: LANES - wide]], axis=0)
        high_half = jnp.concatenate([p[1][LANES - wide :], p[2], zeros, ids], axis=0)
        return jnp.concatenate([low_half, high_half], axis=1).astype(jnp.bfloat16)

    copies = []
    for g in range(0, groups, 2):
        sent = mm(pick, jnp.concatenate([message(g), message(g + 1)], axis=0), NT)
        for i in range(2):
            out_ref[g + i] = sent[:, i * LANES : (i + 1) * LANES].astype(jnp.bfloat16)
        copies.append(fetch(11 + g // 2, out_ref.at[g : g + 2], out_hbm.at[g : g + 2]))
    for copy in copies:
        copy.wait()


def call_pairs(ves_count, groups, live, adj, up, down, radial, dist, owner, local, analysis):
    comps, ves, _ = adj.shape
    fine = up.shape[1]
    pairs = ves * dist.shape[0]
    out = (groups, ves_count * ROWS, LANES)
    like = lambda a: pltpu.VMEM(a.shape, a.dtype)
    return pl.pallas_call(
        pairs_kernel,
        out_shape=jax.ShapeDtypeStruct(out, jnp.bfloat16),
        in_specs=[pl.BlockSpec(memory_space=pl.ANY)] * 9,
        out_specs=pl.BlockSpec(memory_space=pl.ANY),
        scratch_shapes=[
            pltpu.SMEM(live.shape, live.dtype), like(adj), like(up), like(down), pltpu.VMEM((1, fine), jnp.float32),
            like(dist), like(owner), like(local), like(analysis),
            pltpu.VMEM((comps * ves, fine), jnp.float32),
            pltpu.VMEM((comps * pairs, fine), jnp.bfloat16),
            pltpu.VMEM((analysis.shape[0], fine), jnp.bfloat16),
            pltpu.VMEM(out, jnp.bfloat16),
            pltpu.SemaphoreType.DMA((13,)),
        ],
        compiler_params=pltpu.CompilerParams(vmem_limit_bytes=61 * 1024 * 1024),
        name="pairs",
    )(live, adj, up, down, radial, dist, owner, local, analysis)


def self_kernel_body(group_ref, adj_hbm, jac_hbm, kernel_hbm, analysis_hbm, *refs):
    *outs, adj_ref, jac_ref, kernel_ref, analysis_ref, s_ref, sem = refs
    sources = [analysis_hbm, kernel_hbm, adj_hbm, jac_hbm]
    targets = [analysis_ref, kernel_ref, adj_ref, jac_ref]
    copies = [
        pltpu.make_async_copy(source, target, sem.at[i])
        for i, (source, target) in enumerate(zip(sources, targets))
    ]
    for copy in copies:
        copy.start()
    for copy in copies:
        copy.wait()
    comps, ves, points = adj_ref.shape
    groups, wide, _ = s_ref.shape
    high, low = split(analysis_ref[...])
    s = mm(high, kernel_ref[...], NT) + mm(low, kernel_ref[...], NT)
    for g in range(groups):
        s_ref[g] = s[g * wide : (g + 1) * wide]
    scaled = (adj_ref[...].astype(jnp.float32) * jac_ref[...].astype(jnp.float32)[None]).astype(
        jnp.bfloat16
    )
    scaled = scaled.reshape(comps * ves, points)
    for i, out in enumerate(outs):
        s_high, s_low = split(s_ref[(group_ref[0] + i) % groups])
        value = mm(scaled, s_high, NT) + mm(scaled, s_low, NT)
        out[...] = jnp.concatenate(
            [value, jnp.zeros((comps * ves, LANES - wide), jnp.float32)], axis=1
        )


def call_self(groups, group, adj, jac, kernel, analysis):
    comps, ves, points = adj.shape
    vmem = pl.BlockSpec(memory_space=pltpu.VMEM)
    like = lambda a: pltpu.VMEM(a.shape, a.dtype)
    return pl.pallas_call(
        self_kernel_body,
        out_shape=[jax.ShapeDtypeStruct((comps * ves, LANES), jnp.float32)] * groups,
        in_specs=[pl.BlockSpec(memory_space=pltpu.SMEM)] + [pl.BlockSpec(memory_space=pl.ANY)] * 4,
        out_specs=[vmem] * groups,
        scratch_shapes=[
            like(adj), like(jac), like(kernel), like(analysis),
            pltpu.VMEM((groups, analysis.shape[0] // groups, points), jnp.float32),
            pltpu.SemaphoreType.DMA((4,)),
        ],
        compiler_params=pltpu.CompilerParams(vmem_limit_bytes=63 * 1024 * 1024),
        name="self_term",
    )(group, adj, jac, kernel, analysis)


def prepare_kernel(group_ref, blocks_ref, *refs):
    *selfs, self_ref, cofactor_ref, det_ref, order_ref = refs
    groups = len(selfs)
    comps, wide, ves = self_ref.shape
    ves_dev = ves // groups
    group = group_ref[0]
    for i, ref in enumerate(selfs):
        order_ref[(group + groups - i) % groups] = ref[...]
    for c in range(comps):
        own = [order_ref[d, c * ves_dev : (c + 1) * ves_dev] for d in range(groups)]
        self_ref[c] = jnp.concatenate(own, axis=0).T[:wide]
    at = lax.broadcasted_iota(jnp.int32, (wide, ves), 0)
    half = wide // 2

    def spread(r, c):
        b = [jnp.broadcast_to(blocks_ref[r, c, d : d + 1, :], (wide, ves)) for d in range(4)]
        lower = jnp.where(at < 4 * group + 3, b[0], b[1])
        upper = jnp.where(at < 4 * group + 5 + half, b[2], b[3])
        return jnp.where(at < half, lower, upper)

    m = [[spread(r, c) for c in range(3)] for r in range(3)]

    def cofactor(r, c):
        r1, r2, c1, c2 = (r + 1) % 3, (r + 2) % 3, (c + 1) % 3, (c + 2) % 3
        return m[r1][c1] * m[r2][c2] - m[r1][c2] * m[r2][c1]

    first = [cofactor(0, c) for c in range(3)]
    det_ref[...] = m[0][0] * first[0] + m[0][1] * first[1] + m[0][2] * first[2]
    for r in range(3):
        for c in range(3):
            cofactor_ref[r, c] = first[c] if r == 0 else cofactor(r, c)


def call_prepare(wide, group, blocks, selfs):
    comps, ves = blocks.shape[0], blocks.shape[-1]
    vmem = pl.BlockSpec(memory_space=pltpu.VMEM)
    f32 = jnp.float32
    return pl.pallas_call(
        prepare_kernel,
        out_shape=[
            pltpu.VMEM((comps, wide, ves), f32),
            pltpu.VMEM((3, 3, wide, ves), f32),
            pltpu.VMEM((wide, ves), f32),
        ],
        in_specs=[pl.BlockSpec(memory_space=pltpu.SMEM)] + [vmem] * (1 + len(selfs)),
        out_specs=[vmem] * 3,
        scratch_shapes=[pltpu.VMEM((len(selfs),) + selfs[0].shape, f32)],
        compiler_params=pltpu.CompilerParams(vmem_limit_bytes=16 * 1024 * 1024),
        name="prepare",
    )(group, blocks, *selfs)


def solve_kernel(got_ref, self_ref, cofactor_ref, det_ref, out_ref):
    senders, rows, lanes = got_ref.shape
    comps, wide, ves = out_ref.shape
    lane = lax.broadcasted_iota(jnp.int32, (senders, 8, lanes), 2).astype(jnp.float32)
    row = lax.broadcasted_iota(jnp.int32, (senders, 8, lanes), 1)
    first = got_ref[:, 8:16, lanes - 1 : lanes].astype(jnp.float32)
    other = got_ref[:, 16:24, lanes - 1 : lanes].astype(jnp.float32)
    first = jnp.where(first == lane, 1.0, 0.0)
    other = jnp.where(other == lane, 1.0, 0.0)
    zero = jnp.zeros_like(first)
    to_low = [first, zero, jnp.where(row < 4, pltpu.roll(other, 4, 1), 0.0)]
    to_high = [zero, first, jnp.where(row < 4, 0.0, other)]
    flat = got_ref[...].reshape(senders * rows, lanes)

    to = [jnp.concatenate(t, axis=1).reshape(senders * rows, lanes) for t in (to_low, to_high)]
    both = mm(flat, jnp.concatenate(to, axis=1).astype(jnp.bfloat16), TN)
    near_low, near_high = both[:, :lanes], both[:, lanes:]
    cut = 2 * wide - lanes
    near = [
        near_low[:wide],
        jnp.concatenate([near_low[wide:], near_high[:cut]], axis=0),
        near_high[cut : cut + wide],
    ]
    rhs = [(self_ref[c] + near[c]).astype(jnp.bfloat16).astype(jnp.float32) for c in range(comps)]
    det = det_ref[...]
    for c in range(comps):
        out_ref[c] = (
            cofactor_ref[0, c] * rhs[0] + cofactor_ref[1, c] * rhs[1] + cofactor_ref[2, c] * rhs[2]
        ) / det


def call_solve(got, prepared):
    vmem = pl.BlockSpec(memory_space=pltpu.VMEM)
    return pl.pallas_call(
        solve_kernel,
        out_shape=jax.ShapeDtypeStruct(prepared[0].shape, jnp.float32),
        in_specs=[vmem] * (1 + len(prepared)),
        out_specs=vmem,
        compiler_params=pltpu.CompilerParams(vmem_limit_bytes=24 * 1024 * 1024),
        name="solve",
    )(got, *prepared)


def body(
    adj_velocity,
    jacobian,
    self_kernel,
    near_kernel_up,
    near_kernel_down,
    radial,
    near_dist,
    near_owner,
    near_local,
    live_pairs,
    analysis,
    blocks,
):
    ves_count, groups = lax.axis_size("ves"), lax.axis_size("deg")
    group = lax.axis_index("deg").astype(jnp.int32)[None]
    adj = adj_velocity.transpose(1, 0, 2)
    projection = analysis.T
    sent = call_pairs(
        ves_count, groups, live_pairs, adj, near_kernel_up, near_kernel_down.T, radial,
        near_dist.T, near_owner.T, near_local.T, projection,
    )
    sent, late = lax.optimization_barrier((sent, group))
    got = lax.all_to_all(
        sent.reshape(groups * ves_count, ROWS, LANES),
        ("deg", "ves"),
        split_axis=0,
        concat_axis=0,
        tiled=True,
    )
    selfs = call_self(groups, late, adj, jacobian, self_kernel, projection)
    selfs = [selfs[0]] + [
        lax.ppermute(selfs[i], "deg", [(j, (j + i) % groups) for j in range(groups)])
        for i in range(1, groups)
    ]
    wide = analysis.shape[1] // groups
    prepared = call_prepare(wide, group, blocks.transpose(1, 2, 0, 3), selfs)
    return call_solve(got, prepared)


def solution(mesh):
    return jax.shard_map(
        body,
        mesh=mesh,
        in_specs=(
            P(("ves", "deg"), None, None),
            P(("ves", "deg"), None),
            P(),
            P(),
            P(),
            P(),
            P(("ves", "deg"), None),
            P(("ves", "deg"), None),
            P(("ves", "deg"), None),
            P(("ves", "deg")),
            P(),
            P("deg", None, None, "ves"),
        ),
        out_specs=P(None, "deg", "ves"),
        check_vma=False,
    )
```

```python
import jax
import jax.numpy as jnp
from jax import lax
from jax.experimental import pallas as pl
from jax.experimental.pallas import tpu as pltpu
from jax.sharding import PartitionSpec as P

LANES = 128
NN = (((1,), (0,)), ((), ()))
NT = (((1,), (1,)), ((), ()))
TN = (((0,), (0,)), ((), ()))
SLOTS = 12
ROWS = 2 * SLOTS


def mm(a, b, dims=NN):
    return lax.dot_general(a, b, dims, preferred_element_type=jnp.float32)


def split(x):
    high = x.astype(jnp.bfloat16)
    return high, (x - high.astype(jnp.float32)).astype(jnp.bfloat16)


def columns(x, count):
    return jnp.concatenate(
        [jnp.broadcast_to(x[:, v : v + 1], (x.shape[0], LANES)) for v in range(count)], axis=0
    )


def route(dest, ident, ves_count):
    near, ves = dest.shape
    pairs = near * ves
    lane = lax.broadcasted_iota(jnp.int32, (pairs, LANES), 1)
    hot = jnp.where(columns(dest, ves) == lane, 1.0, 0.0)
    earlier = jnp.where(
        lax.broadcasted_iota(jnp.int32, (pairs, pairs), 0)
        > lax.broadcasted_iota(jnp.int32, (pairs, pairs), 1),
        1.0,
        0.0,
    ).astype(jnp.bfloat16)
    counts = mm(earlier, hot.astype(jnp.bfloat16))
    ones = jnp.ones((8, LANES), jnp.bfloat16)
    rank = mm(ones, (hot * counts).astype(jnp.bfloat16), NT)
    place = mm(ones, (hot * (lane + 1).astype(jnp.float32)).astype(jnp.bfloat16), NT)
    ids = jnp.where(lane == 0, columns(ident.astype(jnp.float32), ves), 0.0)
    ids = mm(ones, ids.astype(jnp.bfloat16), NT)
    slot = ((place - 1.0) * SLOTS + rank)[:1]
    row = lax.broadcasted_iota(jnp.int32, (ROWS, pairs), 0)
    tile, inner = row // 8, row % 8
    code = jnp.where(tile == 2, 8 + inner % 4, inner).astype(jnp.float32)
    upper = jnp.where(tile == 2, inner // 4, tile)
    pick = []
    for half in range(2):
        wanted = jnp.where(upper == half, code, 1e6)
        hits = [jnp.where(wanted == slot - k * SLOTS, 1.0, 0.0) for k in range(ves_count)]
        pick.append(jnp.concatenate(hits, axis=0))
    return jnp.concatenate(pick, axis=1).astype(jnp.bfloat16), ids


def pairs_kernel(
    live_hbm, adj_hbm, up_hbm, down_hbm, radial_hbm, dist_hbm, owner_hbm, local_hbm, analysis_hbm,
    out_hbm,
    live_ref, adj_ref, up_ref, down_ref, radial_ref, dist_ref, owner_ref, local_ref, analysis_ref,
    ups_ref, field_ref, m_ref, out_ref, sem,
):
    comps, ves, points = adj_ref.shape
    fine = up_ref.shape[1]
    near = dist_ref.shape[0]
    pairs = near * ves
    groups = out_ref.shape[0]
    ves_count = out_ref.shape[1] // ROWS
    wide = analysis_ref.shape[0] // groups
    half = fine // 2 // 256 * 256

    def fetch(i, source, target):
        copy = pltpu.make_async_copy(source, target, sem.at[i])
        copy.start()
        return copy

    small = [
        fetch(0, owner_hbm, owner_ref),
        fetch(1, local_hbm, local_ref),
        fetch(2, dist_hbm, dist_ref),
        fetch(3, radial_hbm, radial_ref.at[0]),
        fetch(10, live_hbm, live_ref),
    ]
    get_adj = fetch(4, adj_hbm, adj_ref)
    get_up = [fetch(5, up_hbm.at[:, :half], up_ref.at[:, :half])]
    get_analysis = fetch(6, analysis_hbm, analysis_ref)
    get_down = [fetch(7, down_hbm.at[:, :half], down_ref.at[:, :half])]
    for copy in small:
        copy.wait()
    get_up.append(fetch(8, up_hbm.at[:, half:], up_ref.at[:, half:]))
    get_down.append(fetch(9, down_hbm.at[:, half:], down_ref.at[:, half:]))

    owner = owner_ref[...]
    order = lax.broadcasted_iota(jnp.int32, owner.shape, 1) * near + lax.broadcasted_iota(
        jnp.int32, owner.shape, 0
    )
    dest = jnp.where(order < live_ref[0], owner // groups, -1)
    pick, ids = route(dest, (owner % groups) * ves + local_ref[...], ves_count)
    dist = columns(dist_ref[...], ves)
    get_adj.wait()
    adj = adj_ref[...].reshape(comps * ves, points)
    even = points // 256 * 256
    refined = 256 - (points - even)

    def project(start, stop):
        at = slice(start, stop)
        last = jnp.concatenate([down_ref[even:, at], down_ref[:refined, at]], axis=0)
        m_ref[:, at] = (mm(high[:, :even], down_ref[:even, at]) + mm(tails, last)).astype(jnp.bfloat16)

    def fields(start, stop):
        for s in range(start, stop, LANES):
            size = min(LANES, stop - s)
            at = slice(s, s + size)
            weight = 1.0 / (1.0 + dist[:, :size] * radial_ref[:, at])
            for c in range(comps):
                ups = [
                    jnp.broadcast_to(ups_ref[c * ves + v : c * ves + v + 1, at], (near, size))
                    for v in range(ves)
                ]
                value = jnp.concatenate(ups, axis=0) * weight
                field_ref[c * pairs : (c + 1) * pairs, at] = value.astype(jnp.bfloat16)

    for i, (start, stop) in enumerate([(0, half), (half, fine)]):
        get_up[i].wait()
        ups_ref[:, start:stop] = mm(adj, up_ref[:, start:stop])
        if i == 0:
            get_analysis.wait()
            high, low = split(analysis_ref[...])
            tails = jnp.concatenate([high[:, even:], low[:, :refined]], axis=1)
        get_down[i].wait()
        for s in range(start, stop, 256):
            project(s, min(s + 256, stop))
            fields(s, min(s + 256, stop))
    part = mm(m_ref[...], field_ref[...], NT)

    zeros = jnp.zeros((2 * LANES - 3 * wide - 8, pairs), jnp.float32)

    def message(g):
        p = [part[g * wide : (g + 1) * wide, c * pairs : (c + 1) * pairs] for c in range(comps)]
        low_half = jnp.concatenate([p[0], p[1][: LANES - wide]], axis=0)
        high_half = jnp.concatenate([p[1][LANES - wide :], p[2], zeros, ids], axis=0)
        return jnp.concatenate([low_half, high_half], axis=1).astype(jnp.bfloat16)

    copies = []
    for g in range(0, groups, 2):
        sent = mm(pick, jnp.concatenate([message(g), message(g + 1)], axis=0), NT)
        for i in range(2):
            out_ref[g + i] = sent[:, i * LANES : (i + 1) * LANES].astype(jnp.bfloat16)
        copies.append(fetch(11 + g // 2, out_ref.at[g : g + 2], out_hbm.at[g : g + 2]))
    for copy in copies:
        copy.wait()


def call_pairs(ves_count, groups, live, adj, up, down, radial, dist, owner, local, analysis):
    comps, ves, _ = adj.shape
    fine = up.shape[1]
    pairs = ves * dist.shape[0]
    out = (groups, ves_count * ROWS, LANES)
    like = lambda a: pltpu.VMEM(a.shape, a.dtype)
    return pl.pallas_call(
        pairs_kernel,
        out_shape=jax.ShapeDtypeStruct(out, jnp.bfloat16),
        in_specs=[pl.BlockSpec(memory_space=pl.ANY)] * 9,
        out_specs=pl.BlockSpec(memory_space=pl.ANY),
        scratch_shapes=[
            pltpu.SMEM(live.shape, live.dtype), like(adj), like(up), like(down), pltpu.VMEM((1, fine), jnp.float32),
            like(dist), like(owner), like(local), like(analysis),
            pltpu.VMEM((comps * ves, fine), jnp.float32),
            pltpu.VMEM((comps * pairs, fine), jnp.bfloat16),
            pltpu.VMEM((analysis.shape[0], fine), jnp.bfloat16),
            pltpu.VMEM(out, jnp.bfloat16),
            pltpu.SemaphoreType.DMA((13,)),
        ],
        compiler_params=pltpu.CompilerParams(vmem_limit_bytes=61 * 1024 * 1024),
        name="pairs",
    )(live, adj, up, down, radial, dist, owner, local, analysis)


def self_kernel_body(group_ref, adj_hbm, jac_hbm, kernel_hbm, analysis_hbm, *refs):
    *outs, adj_ref, jac_ref, kernel_ref, analysis_ref, s_ref, sem = refs
    sources = [analysis_hbm, kernel_hbm, adj_hbm, jac_hbm]
    targets = [analysis_ref, kernel_ref, adj_ref, jac_ref]
    copies = [
        pltpu.make_async_copy(source, target, sem.at[i])
        for i, (source, target) in enumerate(zip(sources, targets))
    ]
    for copy in copies:
        copy.start()
    for copy in copies:
        copy.wait()
    comps, ves, points = adj_ref.shape
    groups, wide, _ = s_ref.shape
    high, low = split(analysis_ref[...])
    s = mm(high, kernel_ref[...], NT) + mm(low, kernel_ref[...], NT)
    for g in range(groups):
        s_ref[g] = s[g * wide : (g + 1) * wide]
    scaled = (adj_ref[...].astype(jnp.float32) * jac_ref[...].astype(jnp.float32)[None]).astype(
        jnp.bfloat16
    )
    scaled = scaled.reshape(comps * ves, points)
    for i, out in enumerate(outs):
        s_high, s_low = split(s_ref[(group_ref[0] + i) % groups])
        value = mm(scaled, s_high, NT) + mm(scaled, s_low, NT)
        out[...] = jnp.concatenate(
            [value, jnp.zeros((comps * ves, LANES - wide), jnp.float32)], axis=1
        )


def call_self(groups, group, adj, jac, kernel, analysis):
    comps, ves, points = adj.shape
    vmem = pl.BlockSpec(memory_space=pltpu.VMEM)
    like = lambda a: pltpu.VMEM(a.shape, a.dtype)
    return pl.pallas_call(
        self_kernel_body,
        out_shape=[pltpu.VMEM((comps * ves, LANES), jnp.float32)] * groups,
        in_specs=[pl.BlockSpec(memory_space=pltpu.SMEM)] + [pl.BlockSpec(memory_space=pl.ANY)] * 4,
        out_specs=[vmem] * groups,
        scratch_shapes=[
            like(adj), like(jac), like(kernel), like(analysis),
            pltpu.VMEM((groups, analysis.shape[0] // groups, points), jnp.float32),
            pltpu.SemaphoreType.DMA((4,)),
        ],
        compiler_params=pltpu.CompilerParams(vmem_limit_bytes=63 * 1024 * 1024),
        name="self_term",
    )(group, adj, jac, kernel, analysis)


def prepare_kernel(group_ref, blocks_ref, *refs):
    *selfs, self_ref, cofactor_ref, det_ref, order_ref = refs
    groups = len(selfs)
    comps, wide, ves = self_ref.shape
    ves_dev = ves // groups
    group = group_ref[0]
    for i, ref in enumerate(selfs):
        order_ref[(group + groups - i) % groups] = ref[...]
    for c in range(comps):
        own = [order_ref[d, c * ves_dev : (c + 1) * ves_dev] for d in range(groups)]
        self_ref[c] = jnp.concatenate(own, axis=0).T[:wide]
    at = lax.broadcasted_iota(jnp.int32, (wide, ves), 0)
    half = wide // 2

    def spread(r, c):
        b = [jnp.broadcast_to(blocks_ref[r, c, d : d + 1, :], (wide, ves)) for d in range(4)]
        lower = jnp.where(at < 4 * group + 3, b[0], b[1])
        upper = jnp.where(at < 4 * group + 5 + half, b[2], b[3])
        return jnp.where(at < half, lower, upper)

    m = [[spread(r, c) for c in range(3)] for r in range(3)]

    def cofactor(r, c):
        r1, r2, c1, c2 = (r + 1) % 3, (r + 2) % 3, (c + 1) % 3, (c + 2) % 3
        return m[r1][c1] * m[r2][c2] - m[r1][c2] * m[r2][c1]

    first = [cofactor(0, c) for c in range(3)]
    det_ref[...] = m[0][0] * first[0] + m[0][1] * first[1] + m[0][2] * first[2]
    for r in range(3):
        for c in range(3):
            cofactor_ref[r, c] = first[c] if r == 0 else cofactor(r, c)


def call_prepare(wide, group, blocks, selfs):
    comps, ves = blocks.shape[0], blocks.shape[-1]
    vmem = pl.BlockSpec(memory_space=pltpu.VMEM)
    f32 = jnp.float32
    return pl.pallas_call(
        prepare_kernel,
        out_shape=[
            pltpu.VMEM((comps, wide, ves), f32),
            pltpu.VMEM((3, 3, wide, ves), f32),
            pltpu.VMEM((wide, ves), f32),
        ],
        in_specs=[pl.BlockSpec(memory_space=pltpu.SMEM)] + [vmem] * (1 + len(selfs)),
        out_specs=[vmem] * 3,
        scratch_shapes=[pltpu.VMEM((len(selfs),) + selfs[0].shape, f32)],
        compiler_params=pltpu.CompilerParams(vmem_limit_bytes=16 * 1024 * 1024),
        name="prepare",
    )(group, blocks, *selfs)


def solve_kernel(got_ref, self_ref, cofactor_ref, det_ref, out_ref):
    senders, rows, lanes = got_ref.shape
    comps, wide, ves = out_ref.shape
    lane = lax.broadcasted_iota(jnp.int32, (senders, 8, lanes), 2).astype(jnp.float32)
    row = lax.broadcasted_iota(jnp.int32, (senders, 8, lanes), 1)
    first = got_ref[:, 8:16, lanes - 1 : lanes].astype(jnp.float32)
    other = got_ref[:, 16:24, lanes - 1 : lanes].astype(jnp.float32)
    first = jnp.where(first == lane, 1.0, 0.0)
    other = jnp.where(other == lane, 1.0, 0.0)
    zero = jnp.zeros_like(first)
    to_low = [first, zero, jnp.where(row < 4, pltpu.roll(other, 4, 1), 0.0)]
    to_high = [zero, first, jnp.where(row < 4, 0.0, other)]
    flat = got_ref[...].reshape(senders * rows, lanes)

    to = [jnp.concatenate(t, axis=1).reshape(senders * rows, lanes) for t in (to_low, to_high)]
    both = mm(flat, jnp.concatenate(to, axis=1).astype(jnp.bfloat16), TN)
    near_low, near_high = both[:, :lanes], both[:, lanes:]
    cut = 2 * wide - lanes
    near = [
        near_low[:wide],
        jnp.concatenate([near_low[wide:], near_high[:cut]], axis=0),
        near_high[cut : cut + wide],
    ]
    rhs = [(self_ref[c] + near[c]).astype(jnp.bfloat16).astype(jnp.float32) for c in range(comps)]
    det = det_ref[...]
    for c in range(comps):
        out_ref[c] = (
            cofactor_ref[0, c] * rhs[0] + cofactor_ref[1, c] * rhs[1] + cofactor_ref[2, c] * rhs[2]
        ) / det


def call_solve(got, prepared):
    vmem = pl.BlockSpec(memory_space=pltpu.VMEM)
    return pl.pallas_call(
        solve_kernel,
        out_shape=jax.ShapeDtypeStruct(prepared[0].shape, jnp.float32),
        in_specs=[vmem] * (1 + len(prepared)),
        out_specs=vmem,
        compiler_params=pltpu.CompilerParams(vmem_limit_bytes=24 * 1024 * 1024),
        name="solve",
    )(got, *prepared)


def body(
    adj_velocity,
    jacobian,
    self_kernel,
    near_kernel_up,
    near_kernel_down,
    radial,
    near_dist,
    near_owner,
    near_local,
    live_pairs,
    analysis,
    blocks,
):
    ves_count, groups = lax.axis_size("ves"), lax.axis_size("deg")
    group = lax.axis_index("deg").astype(jnp.int32)[None]
    adj = adj_velocity.transpose(1, 0, 2)
    projection = analysis.T
    sent = call_pairs(
        ves_count, groups, live_pairs, adj, near_kernel_up, near_kernel_down.T, radial,
        near_dist.T, near_owner.T, near_local.T, projection,
    )
    sent, late = lax.optimization_barrier((sent, group))
    got = lax.all_to_all(
        sent.reshape(groups * ves_count, ROWS, LANES),
        ("deg", "ves"),
        split_axis=0,
        concat_axis=0,
        tiled=True,
    )
    selfs = call_self(groups, late, adj, jacobian, self_kernel, projection)
    selfs = [selfs[0]] + [
        lax.ppermute(selfs[i], "deg", [(j, (j + i) % groups) for j in range(groups)])
        for i in range(1, groups)
    ]
    wide = analysis.shape[1] // groups
    prepared = call_prepare(wide, group, blocks.transpose(1, 2, 0, 3), selfs)
    return call_solve(got, prepared)


def solution(mesh):
    return jax.shard_map(
        body,
        mesh=mesh,
        in_specs=(
            P(("ves", "deg"), None, None),
            P(("ves", "deg"), None),
            P(),
            P(),
            P(),
            P(),
            P(("ves", "deg"), None),
            P(("ves", "deg"), None),
            P(("ves", "deg"), None),
            P(("ves", "deg")),
            P(),
            P("deg", None, None, "ves"),
        ),
        out_specs=P(None, "deg", "ves"),
        check_vma=False,
    )
```

```python
import jax
import jax.numpy as jnp
from jax import lax
from jax.experimental import pallas as pl
from jax.experimental.pallas import tpu as pltpu
from jax.sharding import PartitionSpec as P

LANES = 128
NN = (((1,), (0,)), ((), ()))
NT = (((1,), (1,)), ((), ()))
TN = (((0,), (0,)), ((), ()))
SLOTS = 12
ROWS = 2 * SLOTS


def mm(a, b, dims=NN):
    return lax.dot_general(a, b, dims, preferred_element_type=jnp.float32)


def split(x):
    high = x.astype(jnp.bfloat16)
    return high, (x - high.astype(jnp.float32)).astype(jnp.bfloat16)


def columns(x, count):
    return jnp.concatenate(
        [jnp.broadcast_to(x[:, v : v + 1], (x.shape[0], LANES)) for v in range(count)], axis=0
    )


def route(dest, ident, ves_count):
    near, ves = dest.shape
    pairs = near * ves
    lane = lax.broadcasted_iota(jnp.int32, (pairs, LANES), 1)
    hot = jnp.where(columns(dest, ves) == lane, 1.0, 0.0)
    earlier = jnp.where(
        lax.broadcasted_iota(jnp.int32, (pairs, pairs), 0)
        > lax.broadcasted_iota(jnp.int32, (pairs, pairs), 1),
        1.0,
        0.0,
    ).astype(jnp.bfloat16)
    counts = mm(earlier, hot.astype(jnp.bfloat16))
    ones = jnp.ones((8, LANES), jnp.bfloat16)
    rank = mm(ones, (hot * counts).astype(jnp.bfloat16), NT)
    place = mm(ones, (hot * (lane + 1).astype(jnp.float32)).astype(jnp.bfloat16), NT)
    ids = jnp.where(lane == 0, columns(ident.astype(jnp.float32), ves), 0.0)
    ids = mm(ones, ids.astype(jnp.bfloat16), NT)
    slot = ((place - 1.0) * SLOTS + rank)[:1]
    row = lax.broadcasted_iota(jnp.int32, (ROWS, pairs), 0)
    tile, inner = row // 8, row % 8
    code = jnp.where(tile == 2, 8 + inner % 4, inner).astype(jnp.float32)
    upper = jnp.where(tile == 2, inner // 4, tile)
    pick = []
    for half in range(2):
        wanted = jnp.where(upper == half, code, 1e6)
        hits = [jnp.where(wanted == slot - k * SLOTS, 1.0, 0.0) for k in range(ves_count)]
        pick.append(jnp.concatenate(hits, axis=0))
    return jnp.concatenate(pick, axis=1).astype(jnp.bfloat16), ids


def pairs_kernel(
    live_hbm, adj_hbm, up_hbm, down_hbm, radial_hbm, dist_hbm, owner_hbm, local_hbm, analysis_hbm,
    out_hbm,
    live_ref, adj_ref, up_ref, down_ref, radial_ref, dist_ref, owner_ref, local_ref, analysis_ref,
    ups_ref, field_ref, m_ref, out_ref, sem,
):
    comps, ves, points = adj_ref.shape
    fine = up_ref.shape[1]
    near = dist_ref.shape[0]
    pairs = near * ves
    groups = out_ref.shape[0]
    ves_count = out_ref.shape[1] // ROWS
    wide = analysis_ref.shape[0] // groups
    half = fine // 2 // 256 * 256

    def fetch(i, source, target):
        copy = pltpu.make_async_copy(source, target, sem.at[i])
        copy.start()
        return copy

    small = [
        fetch(0, owner_hbm, owner_ref),
        fetch(1, local_hbm, local_ref),
        fetch(2, dist_hbm, dist_ref),
        fetch(3, radial_hbm, radial_ref.at[0]),
        fetch(10, live_hbm, live_ref),
    ]
    get_adj = fetch(4, adj_hbm, adj_ref)
    get_up = [fetch(5, up_hbm.at[:, :half], up_ref.at[:, :half])]
    get_analysis = fetch(6, analysis_hbm, analysis_ref)
    get_down = [fetch(7, down_hbm.at[:, :half], down_ref.at[:, :half])]
    for copy in small:
        copy.wait()
    get_up.append(fetch(8, up_hbm.at[:, half:], up_ref.at[:, half:]))
    get_down.append(fetch(9, down_hbm.at[:, half:], down_ref.at[:, half:]))

    owner = owner_ref[...]
    order = lax.broadcasted_iota(jnp.int32, owner.shape, 1) * near + lax.broadcasted_iota(
        jnp.int32, owner.shape, 0
    )
    dest = jnp.where(order < live_ref[0], owner // groups, -1)
    pick, ids = route(dest, (owner % groups) * ves + local_ref[...], ves_count)
    dist = columns(dist_ref[...], ves)
    get_adj.wait()
    adj = adj_ref[...].reshape(comps * ves, points)
    even = points // 256 * 256
    refined = 256 - (points - even)

    def project(start, stop):
        at = slice(start, stop)
        last = jnp.concatenate([down_ref[even:, at], down_ref[:refined, at]], axis=0)
        m_ref[:, at] = (mm(high[:, :even], down_ref[:even, at]) + mm(tails, last)).astype(jnp.bfloat16)

    def fields(start, stop):
        for s in range(start, stop, LANES):
            size = min(LANES, stop - s)
            at = slice(s, s + size)
            weight = 1.0 / (1.0 + dist[:, :size] * radial_ref[:, at])
            for c in range(comps):
                ups = [
                    jnp.broadcast_to(ups_ref[c * ves + v : c * ves + v + 1, at], (near, size))
                    for v in range(ves)
                ]
                value = jnp.concatenate(ups, axis=0) * weight
                field_ref[c * pairs : (c + 1) * pairs, at] = value.astype(jnp.bfloat16)

    for i, (start, stop) in enumerate([(0, half), (half, fine)]):
        get_up[i].wait()
        ups_ref[:, start:stop] = mm(adj, up_ref[:, start:stop])
        if i == 0:
            get_analysis.wait()
            high, low = split(analysis_ref[...])
            tails = jnp.concatenate([high[:, even:], low[:, :refined]], axis=1)
        get_down[i].wait()
        for s in range(start, stop, 256):
            fields(s, min(s + 256, stop))
            project(s, min(s + 256, stop))
    part = mm(m_ref[...], field_ref[...], NT)

    zeros = jnp.zeros((2 * LANES - 3 * wide - 8, pairs), jnp.float32)

    def message(g):
        p = [part[g * wide : (g + 1) * wide, c * pairs : (c + 1) * pairs] for c in range(comps)]
        low_half = jnp.concatenate([p[0], p[1][: LANES - wide]], axis=0)
        high_half = jnp.concatenate([p[1][LANES - wide :], p[2], zeros, ids], axis=0)
        return jnp.concatenate([low_half, high_half], axis=1).astype(jnp.bfloat16)

    copies = []
    for g in range(0, groups, 2):
        sent = mm(pick, jnp.concatenate([message(g), message(g + 1)], axis=0), NT)
        for i in range(2):
            out_ref[g + i] = sent[:, i * LANES : (i + 1) * LANES].astype(jnp.bfloat16)
        copies.append(fetch(11 + g // 2, out_ref.at[g : g + 2], out_hbm.at[g : g + 2]))
    for copy in copies:
        copy.wait()


def call_pairs(ves_count, groups, live, adj, up, down, radial, dist, owner, local, analysis):
    comps, ves, _ = adj.shape
    fine = up.shape[1]
    pairs = ves * dist.shape[0]
    out = (groups, ves_count * ROWS, LANES)
    like = lambda a: pltpu.VMEM(a.shape, a.dtype)
    return pl.pallas_call(
        pairs_kernel,
        out_shape=jax.ShapeDtypeStruct(out, jnp.bfloat16),
        in_specs=[pl.BlockSpec(memory_space=pl.ANY)] * 9,
        out_specs=pl.BlockSpec(memory_space=pl.ANY),
        scratch_shapes=[
            pltpu.SMEM(live.shape, live.dtype), like(adj), like(up), like(down), pltpu.VMEM((1, fine), jnp.float32),
            like(dist), like(owner), like(local), like(analysis),
            pltpu.VMEM((comps * ves, fine), jnp.float32),
            pltpu.VMEM((comps * pairs, fine), jnp.bfloat16),
            pltpu.VMEM((analysis.shape[0], fine), jnp.bfloat16),
            pltpu.VMEM(out, jnp.bfloat16),
            pltpu.SemaphoreType.DMA((13,)),
        ],
        compiler_params=pltpu.CompilerParams(vmem_limit_bytes=61 * 1024 * 1024),
        name="pairs",
    )(live, adj, up, down, radial, dist, owner, local, analysis)


def self_kernel_body(group_ref, adj_hbm, jac_hbm, kernel_hbm, analysis_hbm, *refs):
    *outs, adj_ref, jac_ref, kernel_ref, analysis_ref, s_ref, sem = refs
    sources = [analysis_hbm, kernel_hbm, adj_hbm, jac_hbm]
    targets = [analysis_ref, kernel_ref, adj_ref, jac_ref]
    copies = [
        pltpu.make_async_copy(source, target, sem.at[i])
        for i, (source, target) in enumerate(zip(sources, targets))
    ]
    for copy in copies:
        copy.start()
    for copy in copies:
        copy.wait()
    comps, ves, points = adj_ref.shape
    groups, wide, _ = s_ref.shape
    high, low = split(analysis_ref[...])
    s = mm(high, kernel_ref[...], NT) + mm(low, kernel_ref[...], NT)
    for g in range(groups):
        s_ref[g] = s[g * wide : (g + 1) * wide]
    scaled = (adj_ref[...].astype(jnp.float32) * jac_ref[...].astype(jnp.float32)[None]).astype(
        jnp.bfloat16
    )
    scaled = scaled.reshape(comps * ves, points)
    for i, out in enumerate(outs):
        s_high, s_low = split(s_ref[(group_ref[0] + i) % groups])
        value = mm(scaled, s_high, NT) + mm(scaled, s_low, NT)
        out[...] = jnp.concatenate(
            [value, jnp.zeros((comps * ves, LANES - wide), jnp.float32)], axis=1
        )


def call_self(groups, group, adj, jac, kernel, analysis):
    comps, ves, points = adj.shape
    vmem = pl.BlockSpec(memory_space=pltpu.VMEM)
    like = lambda a: pltpu.VMEM(a.shape, a.dtype)
    return pl.pallas_call(
        self_kernel_body,
        out_shape=[pltpu.VMEM((comps * ves, LANES), jnp.float32)] * groups,
        in_specs=[pl.BlockSpec(memory_space=pltpu.SMEM)] + [pl.BlockSpec(memory_space=pl.ANY)] * 4,
        out_specs=[vmem] * groups,
        scratch_shapes=[
            like(adj), like(jac), like(kernel), like(analysis),
            pltpu.VMEM((groups, analysis.shape[0] // groups, points), jnp.float32),
            pltpu.SemaphoreType.DMA((4,)),
        ],
        compiler_params=pltpu.CompilerParams(vmem_limit_bytes=63 * 1024 * 1024),
        name="self_term",
    )(group, adj, jac, kernel, analysis)


def prepare_kernel(group_ref, blocks_ref, *refs):
    *selfs, self_ref, cofactor_ref, det_ref, order_ref = refs
    groups = len(selfs)
    comps, wide, ves = self_ref.shape
    ves_dev = ves // groups
    group = group_ref[0]
    for i, ref in enumerate(selfs):
        order_ref[(group + groups - i) % groups] = ref[...]
    for c in range(comps):
        own = [order_ref[d, c * ves_dev : (c + 1) * ves_dev] for d in range(groups)]
        self_ref[c] = jnp.concatenate(own, axis=0).T[:wide]
    at = lax.broadcasted_iota(jnp.int32, (wide, ves), 0)
    half = wide // 2

    def spread(r, c):
        b = [jnp.broadcast_to(blocks_ref[r, c, d : d + 1, :], (wide, ves)) for d in range(4)]
        lower = jnp.where(at < 4 * group + 3, b[0], b[1])
        upper = jnp.where(at < 4 * group + 5 + half, b[2], b[3])
        return jnp.where(at < half, lower, upper)

    m = [[spread(r, c) for c in range(3)] for r in range(3)]

    def cofactor(r, c):
        r1, r2, c1, c2 = (r + 1) % 3, (r + 2) % 3, (c + 1) % 3, (c + 2) % 3
        return m[r1][c1] * m[r2][c2] - m[r1][c2] * m[r2][c1]

    first = [cofactor(0, c) for c in range(3)]
    det_ref[...] = m[0][0] * first[0] + m[0][1] * first[1] + m[0][2] * first[2]
    for r in range(3):
        for c in range(3):
            cofactor_ref[r, c] = first[c] if r == 0 else cofactor(r, c)


def call_prepare(wide, group, blocks, selfs):
    comps, ves = blocks.shape[0], blocks.shape[-1]
    vmem = pl.BlockSpec(memory_space=pltpu.VMEM)
    f32 = jnp.float32
    return pl.pallas_call(
        prepare_kernel,
        out_shape=[
            pltpu.VMEM((comps, wide, ves), f32),
            pltpu.VMEM((3, 3, wide, ves), f32),
            pltpu.VMEM((wide, ves), f32),
        ],
        in_specs=[pl.BlockSpec(memory_space=pltpu.SMEM)] + [vmem] * (1 + len(selfs)),
        out_specs=[vmem] * 3,
        scratch_shapes=[pltpu.VMEM((len(selfs),) + selfs[0].shape, f32)],
        compiler_params=pltpu.CompilerParams(vmem_limit_bytes=16 * 1024 * 1024),
        name="prepare",
    )(group, blocks, *selfs)


def solve_kernel(got_ref, self_ref, cofactor_ref, det_ref, out_ref):
    senders, rows, lanes = got_ref.shape
    comps, wide, ves = out_ref.shape
    lane = lax.broadcasted_iota(jnp.int32, (senders, 8, lanes), 2).astype(jnp.float32)
    row = lax.broadcasted_iota(jnp.int32, (senders, 8, lanes), 1)
    first = got_ref[:, 8:16, lanes - 1 : lanes].astype(jnp.float32)
    other = got_ref[:, 16:24, lanes - 1 : lanes].astype(jnp.float32)
    first = jnp.where(first == lane, 1.0, 0.0)
    other = jnp.where(other == lane, 1.0, 0.0)
    zero = jnp.zeros_like(first)
    to_low = [first, zero, jnp.where(row < 4, pltpu.roll(other, 4, 1), 0.0)]
    to_high = [zero, first, jnp.where(row < 4, 0.0, other)]
    flat = got_ref[...].reshape(senders * rows, lanes)

    to = [jnp.concatenate(t, axis=1).reshape(senders * rows, lanes) for t in (to_low, to_high)]
    both = mm(flat, jnp.concatenate(to, axis=1).astype(jnp.bfloat16), TN)
    near_low, near_high = both[:, :lanes], both[:, lanes:]
    cut = 2 * wide - lanes
    near = [
        near_low[:wide],
        jnp.concatenate([near_low[wide:], near_high[:cut]], axis=0),
        near_high[cut : cut + wide],
    ]
    rhs = [(self_ref[c] + near[c]).astype(jnp.bfloat16).astype(jnp.float32) for c in range(comps)]
    det = det_ref[...]
    for c in range(comps):
        out_ref[c] = (
            cofactor_ref[0, c] * rhs[0] + cofactor_ref[1, c] * rhs[1] + cofactor_ref[2, c] * rhs[2]
        ) / det


def call_solve(got, prepared):
    vmem = pl.BlockSpec(memory_space=pltpu.VMEM)
    return pl.pallas_call(
        solve_kernel,
        out_shape=jax.ShapeDtypeStruct(prepared[0].shape, jnp.float32),
        in_specs=[vmem] * (1 + len(prepared)),
        out_specs=vmem,
        compiler_params=pltpu.CompilerParams(vmem_limit_bytes=24 * 1024 * 1024),
        name="solve",
    )(got, *prepared)


def body(
    adj_velocity,
    jacobian,
    self_kernel,
    near_kernel_up,
    near_kernel_down,
    radial,
    near_dist,
    near_owner,
    near_local,
    live_pairs,
    analysis,
    blocks,
):
    ves_count, groups = lax.axis_size("ves"), lax.axis_size("deg")
    group = lax.axis_index("deg").astype(jnp.int32)[None]
    adj = adj_velocity.transpose(1, 0, 2)
    projection = analysis.T
    sent = call_pairs(
        ves_count, groups, live_pairs, adj, near_kernel_up, near_kernel_down.T, radial,
        near_dist.T, near_owner.T, near_local.T, projection,
    )
    sent, late = lax.optimization_barrier((sent, group))
    got = lax.all_to_all(
        sent.reshape(groups * ves_count, ROWS, LANES),
        ("deg", "ves"),
        split_axis=0,
        concat_axis=0,
        tiled=True,
    )
    selfs = call_self(groups, late, adj, jacobian, self_kernel, projection)
    selfs = [selfs[0]] + [
        lax.ppermute(selfs[i], "deg", [(j, (j + i) % groups) for j in range(groups)])
        for i in range(1, groups)
    ]
    wide = analysis.shape[1] // groups
    prepared = call_prepare(wide, group, blocks.transpose(1, 2, 0, 3), selfs)
    return call_solve(got, prepared)


def solution(mesh):
    return jax.shard_map(
        body,
        mesh=mesh,
        in_specs=(
            P(("ves", "deg"), None, None),
            P(("ves", "deg"), None),
            P(),
            P(),
            P(),
            P(),
            P(("ves", "deg"), None),
            P(("ves", "deg"), None),
            P(("ves", "deg"), None),
            P(("ves", "deg")),
            P(),
            P("deg", None, None, "ves"),
        ),
        out_specs=P(None, "deg", "ves"),
        check_vma=False,
    )
```
